32 devices in a mesh: dp: 4 (over y, x), expert: 8 (over z, core).
Axes of the slice: x: 2, y: 2, z: 4, core: 2. Of those that a mesh axis runs over, the one named last changes fastest.
Arguments:
- tokens: bfloat16 [64, 4096], P('expert', 'dp'), may hold values from -6 to 6
- output_gradient: bfloat16 [64, 4096], P('expert', 'dp'), may hold values from -6 to 6
- routes: int32 [64, 2], P('expert'), may hold values from 0 to 3, all different within a row; in each aligned block of 8 rows (0 to 7, 8 to 15, ...) at most 8 rows name the same one
- router_expert_weight: bfloat16 [64, 2], P('expert'), may hold values from 0.049804688 to 0.5
- tenant: int32 [64], P('expert'), may hold values from 0 to 3
- gate_weight: bfloat16 [8, 4096, 512], P('expert', 'dp'), may hold values from -0.09375 to 0.09375
- up_weight: bfloat16 [8, 4096, 512], P('expert', 'dp'), may hold values from -0.09375 to 0.09375
- down_weight: bfloat16 [8, 512, 4096], P('expert', None, 'dp'), may hold values from -0.09375 to 0.09375
- adapter_input_maps: bfloat16 [8, 4096, 2, 4, 8], P('expert', 'dp'), may hold values from -0.09375 to 0.09375
- adapter_output_maps: bfloat16 [8, 2, 4, 16, 512], P('expert'), may hold values from -0.359375 to 0.359375
Outputs:
- input_grad: bfloat16 [64, 4096], P('expert', 'dp')
- adapter_a_grad: float32 [8, 4096, 2, 4, 8], P('expert', 'dp')
- adapter_b_grad: float32 [8, 2, 4, 16, 512], P('expert')
The draws below stay inside these ranges and needn't reach their ends.
Inputs may be any that keep to these rules, and one draw needn't show every extreme that they name: `routes`: among the 8 tokens of each aligned block of rows (the tokens of one index of the expert axis), no expert is chosen more than 8 times, a bound that some block reaches; a token's choices are distinct.
All inputs are finite; a program needn't handle non-finite values.
Results may differ from the reference program's by a relative error of at most 0.0065.
Values may be sent and summed in bfloat16 or wider, within the bound.
No kernel may reach another device: no remote copies, remote signals or barrier semaphores. Data moves between devices by JAX's collectives and lax.ppermute only.
A program may use at most 64 MiB of HBM per device.

```python
import math
import jax
import jax.numpy as jnp
import numpy as np
from jax import lax

MODEL_WIDTH = 4096
EXPERT_HIDDEN = 1024
ADAPTER_RANK = 16
TENANT_COUNT = 4
TOK_COL = 8
ROUTED_EXPERTS = 4
TOPK = 2
CAP = 8
TOKENS = 64
N_EXPERT = 8


def touch_ends(result, key, least, largest):
    index_at = [jax.random.randint(jax.random.fold_in(key, axis), (), 0, length) for axis, length in enumerate(result.shape)]
    widest = result.shape.index(max(result.shape))
    next_to = index_at[:widest] + [(index_at[widest] + 1) % result.shape[widest]] + index_at[widest + 1:]
    return result.at[tuple(index_at)].set(least).at[tuple(next_to)].set(largest)


def steps_of(stream_key, dims, cuts, low, high):
    def one(axis_at, parts):
        steps = jax.random.uniform(jax.random.fold_in(jax.random.fold_in(stream_key, 6), axis_at), (parts,), jnp.float32, low / len(cuts), high / len(cuts))
        return jnp.repeat(jnp.exp(steps), dims[axis_at] // parts).reshape((-1,) + (1,) * (len(dims) - axis_at - 1))

    level = one(*cuts[0])
    for cut in cuts[1:]:
        level = level * one(*cut)
    return level


def deal_out(key, own, number, rows, number_of, top, reach, slope):
    sequence = jax.random.permutation(key, number_of)
    heavy_load, common = portions_of(number_of, rows * top, reach, slope, True), portions_of(number_of, rows * top, reach, slope, False)
    places = jnp.arange(number_of)

    def named(lengths, offset_by):
        used = int((lengths > 0).sum())
        fixed = max(1, used // 4)
        shifted = fixed + (places - fixed + offset_by * (used - fixed)) % max(1, number_of - fixed)
        return jnp.zeros((number_of,), jnp.int32).at[sequence[jnp.where(places < fixed, places, shifted)]].set(jnp.asarray(lengths, jnp.int32))

    lengths = jnp.where(number % 4 == 0, named(heavy_load, number // 4), named(common, number - number // 4 - 1))
    mixed = jax.random.permutation(jax.random.fold_in(own, 3), number_of)
    giver, taker = mixed[0:number_of // 2 * 2:2], mixed[1:number_of // 2 * 2:2]
    margin = jnp.minimum(lengths[giver] - 1, reach - lengths[taker]) // 2
    margin = jnp.where((giver == sequence[0]) | (taker == sequence[0]) | (lengths[taker] == 0), 0, jnp.maximum(margin, 0))
    shifted = jax.random.randint(jax.random.fold_in(own, 4), (number_of // 2,), 0, 1 << 20) % (margin + 1)
    lengths = lengths.at[giver].add(-shifted).at[taker].add(shifted)
    items = jnp.searchsorted(jnp.cumsum(lengths), jnp.arange(rows * top), side="right").astype(jnp.int32)
    listing = items.reshape(top, rows).T
    listing = listing[jax.random.permutation(jax.random.fold_in(own, 1), rows)]
    offset_by = jax.random.randint(jax.random.fold_in(own, 2), (rows, 1), 0, top)
    return jnp.take_along_axis(listing, (jnp.arange(top)[None, :] + offset_by) % top, axis=1)


def portions_of(amount, total, most, skew, full):
    portions = [(1 << 20) // math.isqrt(grade ** skew) + 1 for grade in range(1, amount + 1)]
    largest = most if full else min(most, max(-(-total // amount), total * portions[0] // sum(portions)))
    least = 1 if total - largest >= amount - 1 else 0
    holding, rest = [largest] + [least] * (amount - 1), total - largest - least * (amount - 1)
    while rest > 0:
        free = [i for i in range(1, amount) if holding[i] < largest] or [i for i in range(1, amount) if holding[i] < most]
        whole, left = sum([portions[i] for i in free]), rest
        for i in free:
            more = min(most - holding[i], max(1, left * portions[i] // whole), rest)
            holding[i] = holding[i] + more
            rest = rest - more
    return np.array(holding)


def centred(own_key, dims, scale, bound, split=(), kind=jnp.bfloat16):
    entries = jax.random.normal(own_key, dims, jnp.float32) * scale
    if len(split) > 0:
        entries = steps_of(own_key, dims, split, -0.22, 0.18) * entries
    return jnp.clip(entries, min=-bound, max=bound).astype(kind)


def setup_inputs(seed: int = 0) -> dict:
    keys = jax.random.split(jax.random.key(seed), 11)
    tokens = centred(keys[0], (TOKENS, MODEL_WIDTH), 1.0, 6.0, ((0, 8), (1, 4)))
    output_gradient = centred(keys[1], (TOKENS, MODEL_WIDTH), 1.0, 6.0, ((0, 8), (1, 4)))
    routes_keys = jax.random.split(jax.random.fold_in(keys[2], 1), TOKENS // TOK_COL)
    routes_turns = jax.random.permutation(jax.random.fold_in(keys[2], 3), TOKENS // TOK_COL)
    routes = jax.vmap(lambda own, number: deal_out(jax.random.fold_in(keys[2], 2), own, number, TOK_COL, ROUTED_EXPERTS, TOPK, CAP, 2))(routes_keys, routes_turns).reshape((TOKENS, TOPK))
    router_expert_weight = jnp.clip(0.049804688 + 0.4501953 * jax.random.uniform(keys[3], (TOKENS, TOPK), jnp.float32) ** steps_of(keys[3], (TOKENS, TOPK), ((0, 8),), -0.2, 0.2), 0.049804688, 0.5).astype(jnp.bfloat16)
    tenant = touch_ends(jax.random.randint(keys[4], (TOKENS,), 0, TENANT_COUNT), jax.random.fold_in(keys[4], 1), 0, TENANT_COUNT - 1).astype(jnp.int32)
    gate_weight = centred(keys[5], (N_EXPERT, MODEL_WIDTH, EXPERT_HIDDEN // 2), MODEL_WIDTH ** -0.5, 0.09375, ((0, 8), (1, 4)))
    up_weight = centred(keys[6], (N_EXPERT, MODEL_WIDTH, EXPERT_HIDDEN // 2), MODEL_WIDTH ** -0.5, 0.09375, ((0, 8), (1, 4)))
    down_weight = centred(keys[7], (N_EXPERT, EXPERT_HIDDEN // 2, MODEL_WIDTH), MODEL_WIDTH ** -0.5, 0.09375, ((0, 8), (2, 4)))
    adapter_input_maps = centred(keys[8], (N_EXPERT, MODEL_WIDTH, 2, TENANT_COUNT, ADAPTER_RANK // 2), MODEL_WIDTH ** -0.5, 0.09375, ((0, 8), (1, 4)))
    adapter_output_maps = centred(keys[9], (N_EXPERT, 2, TENANT_COUNT, ADAPTER_RANK, EXPERT_HIDDEN // 2), 0.06, 0.359375, ((0, 8),))
    return dict(tokens=tokens, output_gradient=output_gradient, routes=routes, router_expert_weight=router_expert_weight, tenant=tenant, gate_weight=gate_weight, up_weight=up_weight, down_weight=down_weight, adapter_input_maps=adapter_input_maps, adapter_output_maps=adapter_output_maps)


ADAPTER_SCALE = 2.0


def product_leading(left, right):
    return lax.dot_general(left, right, (((0,), (0,)), ((), ())), preferred_element_type=jnp.float32)


def product_trailing(left, right):
    return lax.dot_general(left, right, (((1,), (1,)), ((), ())), preferred_element_type=jnp.float32)


def spread(values, tenant_mask):
    count = values.shape[0]
    wide = tenant_mask[:, None, :, None] * values.astype(jnp.float32).reshape(count, 2, 1, ADAPTER_RANK)
    return wide.reshape(count, 2, TENANT_COUNT * ADAPTER_RANK).astype(jnp.bfloat16)


def reference(tokens, output_gradient, routes, router_expert_weight, tenant, gate_weight, up_weight, down_weight, adapter_input_maps, adapter_output_maps):
    assigns = TOK_COL * TOPK
    flat_route = routes.reshape(N_EXPERT, assigns).astype(jnp.int32)
    expert_hot = (flat_route[:, :, None] == jnp.arange(ROUTED_EXPERTS, dtype=jnp.int32)[None, None, :]).astype(jnp.int32)
    earlier = jnp.cumsum(expert_hot, axis=1) - expert_hot
    position = jnp.sum(earlier * expert_hot, axis=2).astype(jnp.int32)
    column = jnp.broadcast_to(jnp.arange(N_EXPERT, dtype=jnp.int32)[:, None], (N_EXPERT, assigns))
    token_ids = (column * TOK_COL + (jnp.arange(assigns, dtype=jnp.int32) // TOPK)[None, :]).astype(jnp.int32)
    prob_flat = router_expert_weight.astype(jnp.float32).reshape(N_EXPERT, assigns)
    tenant_flat = tenant[token_ids]
    slot_token = jnp.full((ROUTED_EXPERTS, N_EXPERT, CAP), TOKENS, jnp.int32).at[flat_route, column, position].set(token_ids)
    slot_prob = jnp.zeros((ROUTED_EXPERTS, N_EXPERT, CAP), jnp.float32).at[flat_route, column, position].set(prob_flat)
    slot_tenant = jnp.full((ROUTED_EXPERTS, N_EXPERT, CAP), TENANT_COUNT, jnp.int32).at[flat_route, column, position].set(tenant_flat)
    padded_x = jnp.concatenate([tokens, jnp.zeros((1, MODEL_WIDTH), tokens.dtype)], axis=0)
    padded_dy = jnp.concatenate([output_gradient, jnp.zeros((1, MODEL_WIDTH), output_gradient.dtype)], axis=0)
    hidden_halfway = EXPERT_HIDDEN // 2
    rank_halfway = ADAPTER_RANK // 2

    def one_expert(operands):
        slot_ids, probs, tenants_of, gate_halves, up_halves, down_halves, a_halves, b_halves = operands
        gate_matrix = jnp.concatenate([gate_halves[0], gate_halves[1]], axis=1)
        up_matrix = jnp.concatenate([up_halves[0], up_halves[1]], axis=1)
        weight_down = jnp.concatenate([down_halves[0], down_halves[1]], axis=0)
        adapter_cols = jnp.concatenate([a_halves[0], a_halves[1]], axis=-1).reshape(MODEL_WIDTH, 2 * TENANT_COUNT * ADAPTER_RANK)
        adapter_b = jnp.concatenate([b_halves[0], b_halves[1]], axis=-1)
        gate_output_map = adapter_b[0].reshape(TENANT_COUNT * ADAPTER_RANK, EXPERT_HIDDEN)
        up_output_map = adapter_b[1].reshape(TENANT_COUNT * ADAPTER_RANK, EXPERT_HIDDEN)
        input_rows = padded_x[slot_ids]
        rows_dy = padded_dy[slot_ids]
        count = slot_ids.shape[0]
        tenant_mask = (tenants_of[:, None] == jnp.arange(TENANT_COUNT, dtype=jnp.int32)[None, :]).astype(jnp.float32)
        proj_all = jnp.dot(input_rows, adapter_cols, preferred_element_type=jnp.float32).reshape(count, 2, TENANT_COUNT, ADAPTER_RANK)
        proj_low = jnp.sum(proj_all * tenant_mask[:, None, :, None], axis=2).astype(jnp.bfloat16)
        projection_spread = spread(proj_low, tenant_mask)
        gate_preactivation = jnp.dot(input_rows, gate_matrix, preferred_element_type=jnp.float32) + ADAPTER_SCALE * jnp.dot(projection_spread[:, 0], gate_output_map, preferred_element_type=jnp.float32)
        up_preactivation = jnp.dot(input_rows, up_matrix, preferred_element_type=jnp.float32) + ADAPTER_SCALE * jnp.dot(projection_spread[:, 1], up_output_map, preferred_element_type=jnp.float32)
        act_grad = probs[:, None] * product_trailing(rows_dy, weight_down)
        gate_sig = jax.nn.sigmoid(gate_preactivation)
        gate_gradient = (act_grad * up_preactivation * gate_sig * (1.0 + gate_preactivation * (1.0 - gate_sig))).astype(jnp.bfloat16)
        up_gradient = (act_grad * gate_preactivation * gate_sig).astype(jnp.bfloat16)
        output_map_gradient = ADAPTER_SCALE * jnp.stack([product_leading(projection_spread[:, 0], gate_gradient), product_leading(projection_spread[:, 1], up_gradient)])
        backward_total = ADAPTER_SCALE * jnp.stack([product_trailing(gate_gradient, gate_output_map), product_trailing(up_gradient, up_output_map)], axis=1)
        back_low = jnp.sum(backward_total.reshape(count, 2, TENANT_COUNT, ADAPTER_RANK) * tenant_mask[:, None, :, None], axis=2).astype(jnp.bfloat16)
        back_spread = spread(back_low, tenant_mask).reshape(count, 2 * TENANT_COUNT * ADAPTER_RANK)
        grad_a = product_leading(input_rows, back_spread).reshape(MODEL_WIDTH, 2, TENANT_COUNT, ADAPTER_RANK)
        slot_grad = (product_trailing(gate_gradient, gate_matrix) + product_trailing(up_gradient, up_matrix) + product_trailing(back_spread, adapter_cols)).astype(jnp.bfloat16)
        return slot_grad, grad_a, output_map_gradient.reshape(2, TENANT_COUNT, ADAPTER_RANK, EXPERT_HIDDEN)

    operands = (
        slot_token.reshape(ROUTED_EXPERTS, N_EXPERT * CAP),
        slot_prob.reshape(ROUTED_EXPERTS, N_EXPERT * CAP),
        slot_tenant.reshape(ROUTED_EXPERTS, N_EXPERT * CAP),
        gate_weight.reshape(ROUTED_EXPERTS, 2, MODEL_WIDTH, hidden_halfway),
        up_weight.reshape(ROUTED_EXPERTS, 2, MODEL_WIDTH, hidden_halfway),
        down_weight.reshape(ROUTED_EXPERTS, 2, hidden_halfway, MODEL_WIDTH),
        adapter_input_maps.reshape(ROUTED_EXPERTS, 2, MODEL_WIDTH, 2, TENANT_COUNT, rank_halfway),
        adapter_output_maps.reshape(ROUTED_EXPERTS, 2, 2, TENANT_COUNT, ADAPTER_RANK, hidden_halfway),
    )
    slot_grads, grads_a, grads_b = lax.map(one_expert, operands)
    total = jnp.zeros((TOKENS + 1, MODEL_WIDTH), jnp.float32).at[slot_token.reshape(-1)].add(slot_grads.reshape(-1, MODEL_WIDTH).astype(jnp.float32))
    input_grad = total[:TOKENS].astype(jnp.bfloat16)
    adapter_a_grad = grads_a.reshape(ROUTED_EXPERTS, MODEL_WIDTH, 2, TENANT_COUNT, 2, rank_halfway).transpose(0, 4, 1, 2, 3, 5).reshape(N_EXPERT, MODEL_WIDTH, 2, TENANT_COUNT, rank_halfway)
    adapter_b_grad = grads_b.reshape(ROUTED_EXPERTS, 2, TENANT_COUNT, ADAPTER_RANK, 2, hidden_halfway).transpose(0, 4, 1, 2, 3, 5).reshape(N_EXPERT, 2, TENANT_COUNT, ADAPTER_RANK, hidden_halfway)
    return input_grad, adapter_a_grad, adapter_b_grad
```

```python
import functools

import jax
import jax.numpy as jnp
from jax import lax
from jax.experimental import pallas as pl
from jax.experimental.pallas import tpu as pltpu
from jax.sharding import PartitionSpec as P

ADAPTER_SCALE = 2.0


def partner(shard, axis, bit):
    return lax.ppermute(shard, axis, [(i, i ^ 1 << bit) for i in range(lax.axis_size(axis))])


def product_leading(left, right):
    return lax.dot_general(
        left, right, (((0,), (0,)), ((), ())), preferred_element_type=jnp.float32
    )


def product_trailing(left, right):
    return lax.dot_general(
        left, right, (((1,), (1,)), ((), ())), preferred_element_type=jnp.float32
    )


def order_halves(mine, other, upper):
    return (jnp.where(upper, other, mine), jnp.where(upper, mine, other))


def spread(values, tenant_mask, tenant_list, adapter_rank_width):
    count = values.shape[0]
    wide = tenant_mask[:, None, :, None] * values.astype(jnp.float32).reshape(
        count, 2, 1, adapter_rank_width
    )
    return wide.reshape(count, 2, tenant_list * adapter_rank_width).astype(jnp.bfloat16)


def routed_shards(
    tokens,
    output_gradient,
    routes,
    router_expert_weight,
    tenant,
    gate_weight,
    up_weight,
    down_weight,
    adapter_input_maps,
    adapter_output_maps,
):
    devices = lax.axis_size("expert")
    experts = devices // 2
    tok_col, quarter = tokens.shape
    topk = routes.shape[1]
    tenant_list = adapter_output_maps.shape[2]
    adapter_rank_width = adapter_output_maps.shape[3]
    hidden_halfway = adapter_output_maps.shape[4]
    rank_halfway = adapter_rank_width // 2
    capacity = 2 * tok_col * topk // experts
    half_cap = capacity // 2
    slots = devices * capacity
    upper = lax.axis_index("expert") % 2 == 1
    flat_route = routes.reshape(-1)
    expert_hot = (flat_route[:, None] == jnp.arange(experts, dtype=jnp.int32)[None, :]).astype(
        jnp.int32
    )
    earlier = jnp.cumsum(expert_hot, axis=0) - expert_hot
    position = jnp.sum(earlier * expert_hot, axis=1)
    slot_of = (flat_route * capacity + position).reshape(tok_col, topk)
    slot_range = jnp.arange(experts * capacity, dtype=jnp.int32)
    hits = (slot_range[:, None, None] == slot_of[None, :, :]).astype(jnp.float32)
    select_tok = jnp.sum(hits, axis=2)
    prob_tok = jnp.sum(hits * router_expert_weight.astype(jnp.float32)[None, :, :], axis=2)
    tenant_hot = (tenant[:, None] == jnp.arange(tenant_list, dtype=jnp.int32)[None, :]).astype(
        jnp.float32
    )
    select_bf = select_tok.astype(jnp.bfloat16)
    send_rows = jnp.dot(select_bf, tokens, preferred_element_type=jnp.float32).astype(jnp.bfloat16)
    send_grad = jnp.dot(select_bf, output_gradient, preferred_element_type=jnp.float32).astype(
        jnp.bfloat16
    )
    send_tag = jnp.dot(prob_tok, tenant_hot, precision=lax.Precision.HIGHEST).astype(jnp.bfloat16)

    def doubled(block):
        wide = block.reshape(experts, 1, capacity, block.shape[1])
        return jnp.broadcast_to(wide, (experts, 2, capacity, block.shape[1])).reshape(
            devices, capacity, block.shape[1]
        )

    got_rows, got_grad, got_tag = (
        lax.all_to_all(doubled(send_rows), "expert", split_axis=0, concat_axis=0, tiled=True),
        lax.all_to_all(doubled(send_grad), "expert", split_axis=0, concat_axis=0, tiled=True),
        lax.all_to_all(doubled(send_tag), "expert", split_axis=0, concat_axis=0, tiled=True),
    )
    input_rows = got_rows.reshape(slots, quarter)
    rows_dy = got_grad.reshape(slots, quarter)
    tags = got_tag.reshape(slots, tenant_list).astype(jnp.float32)
    tenant_mask = (tags > 0).astype(jnp.float32)
    slot_prob = jnp.sum(tags, axis=1)
    adapter_local = adapter_input_maps[0]
    adapter_other = partner(adapter_local, "expert", 0)
    low_rank, high_rank = order_halves(adapter_local, adapter_other, upper)
    adapter_cols = jnp.concatenate([low_rank, high_rank], axis=-1).reshape(
        quarter, 2 * tenant_list * adapter_rank_width
    )
    gate_output_map = adapter_output_maps[0, 0].reshape(
        tenant_list * adapter_rank_width, hidden_halfway
    )
    up_output_map = adapter_output_maps[0, 1].reshape(
        tenant_list * adapter_rank_width, hidden_halfway
    )
    gate_part = jnp.dot(input_rows, gate_weight[0], preferred_element_type=jnp.float32)
    up_part = jnp.dot(input_rows, up_weight[0], preferred_element_type=jnp.float32)
    act_part = product_trailing(rows_dy, down_weight[0])
    proj_all = jnp.dot(input_rows, adapter_cols, preferred_element_type=jnp.float32).reshape(
        slots, 2, tenant_list, adapter_rank_width
    )
    proj_part = jnp.sum(proj_all * tenant_mask[:, None, :, None], axis=2).reshape(
        slots, 2 * adapter_rank_width
    )
    gate_total, up_total, act_sum, proj_sum = lax.psum(
        (gate_part, up_part, act_part, proj_part), "dp"
    )
    proj_low = proj_sum.astype(jnp.bfloat16)
    spread_in = spread(proj_low, tenant_mask, tenant_list, adapter_rank_width)
    gate_preactivation = gate_total + ADAPTER_SCALE * jnp.dot(
        spread_in[:, 0], gate_output_map, preferred_element_type=jnp.float32
    )
    up_preactivation = up_total + ADAPTER_SCALE * jnp.dot(
        spread_in[:, 1], up_output_map, preferred_element_type=jnp.float32
    )
    act_grad = slot_prob[:, None] * act_sum
    gate_sig = jax.nn.sigmoid(gate_preactivation)
    gate_gradient = (
        act_grad * up_preactivation * gate_sig * (1.0 + gate_preactivation * (1.0 - gate_sig))
    ).astype(jnp.bfloat16)
    up_gradient = (act_grad * gate_preactivation * gate_sig).astype(jnp.bfloat16)
    gate_gradient, up_gradient, proj_low = (gate_gradient, up_gradient, proj_low)
    projection_spread = spread(proj_low, tenant_mask, tenant_list, adapter_rank_width)
    gate_output_map_gradient = ADAPTER_SCALE * product_leading(
        projection_spread[:, 0], gate_gradient
    )
    up_output_map_gradient = ADAPTER_SCALE * product_leading(projection_spread[:, 1], up_gradient)
    adapter_b_grad = jnp.stack([gate_output_map_gradient, up_output_map_gradient]).reshape(
        1, 2, tenant_list, adapter_rank_width, hidden_halfway
    )
    backward_total = ADAPTER_SCALE * jnp.stack(
        [
            product_trailing(gate_gradient, gate_output_map),
            product_trailing(up_gradient, up_output_map),
        ],
        axis=1,
    )
    back_part = jnp.sum(
        backward_total.reshape(slots, 2, tenant_list, adapter_rank_width)
        * tenant_mask[:, None, :, None],
        axis=2,
    ).reshape(slots, 2 * adapter_rank_width)
    input_part = product_trailing(gate_gradient, gate_weight[0]) + product_trailing(
        up_gradient, up_weight[0]
    )
    by_source = input_part.reshape(devices, capacity, quarter)
    first_half = by_source[:, :half_cap]
    second_half = by_source[:, half_cap:]
    keep_half = jnp.where(upper, second_half, first_half)
    give_half = jnp.where(upper, first_half, second_half)
    taken_half, back_other = partner((give_half, back_part), "expert", 0)
    input_half = keep_half + taken_half
    back_low = (back_part + back_other).astype(jnp.bfloat16)
    back_spread = spread(back_low, tenant_mask, tenant_list, adapter_rank_width)
    spread_rows = back_spread.reshape(devices, capacity, 2 * tenant_list * adapter_rank_width)
    spread_half = jnp.where(upper, spread_rows[:, half_cap:], spread_rows[:, :half_cap]).reshape(
        devices * half_cap, 2 * tenant_list * adapter_rank_width
    )
    adapter_term = product_trailing(spread_half, adapter_cols).reshape(devices, half_cap, quarter)
    slot_grad = (input_half + adapter_term).astype(jnp.bfloat16)
    spread_ranks = back_spread.reshape(slots, 2, tenant_list, adapter_rank_width)
    mine_cols = jnp.where(
        upper, spread_ranks[..., rank_halfway:], spread_ranks[..., :rank_halfway]
    ).reshape(slots, 2 * tenant_list * rank_halfway)
    adapter_a_grad = product_leading(input_rows, mine_cols).reshape(
        1, quarter, 2, tenant_list, rank_halfway
    )
    returned = lax.all_to_all(slot_grad, "expert", split_axis=0, concat_axis=0, tiled=True)
    slot_rows = returned.reshape(experts * capacity, quarter)
    input_grad = product_leading(select_bf, slot_rows).astype(jnp.bfloat16)
    return (input_grad, adapter_a_grad, adapter_b_grad)


F32 = jnp.float32
BF16 = jnp.bfloat16
VMEM = pl.BlockSpec(memory_space=pltpu.VMEM)


def local_call(body, outs, operands, scratch=(), flops=0, moved=0):
    return pl.pallas_call(
        body,
        out_shape=[jax.ShapeDtypeStruct(shape, kind) for shape, kind in outs],
        in_specs=[VMEM] * len(operands),
        out_specs=[VMEM] * len(outs),
        scratch_shapes=list(scratch),
        cost_estimate=pl.CostEstimate(flops=flops, bytes_accessed=moved, transcendentals=0),
    )(*operands)


def dot_plain(left, right):
    return lax.dot_general(left, right, (((1,), (0,)), ((), ())), preferred_element_type=F32)


def swap(array, axis, offset):
    return lax.ppermute(array, axis, [(i, i ^ offset) for i in range(lax.axis_size(axis))])


def pack_body(x_ref, dy_ref, routes_ref, weight_ref, tenant_ref, out_ref):
    width = x_ref.shape[1]
    topk, count = routes_ref.shape
    out_ref[:, :width] = x_ref[...]
    out_ref[:, width : 2 * width] = dy_ref[...]
    tags = [routes_ref[...].astype(F32), weight_ref[...].astype(F32), tenant_ref[...].astype(F32)]
    rows = 2 * topk + 1
    tags = jnp.concatenate(tags + [jnp.zeros((count - rows, count), F32)], axis=0)
    tags = jnp.concatenate([tags, jnp.zeros((count, 128 - count), F32)], axis=1)
    out_ref[:, 2 * width :] = tags.astype(BF16)


def forward_body(topk, *refs):
    blocks = [ref[...].astype(F32) for ref in refs[:-12]]
    gate_ref, up_ref, down_ref, mine_ref, other_ref = refs[-12:-7]
    own_ref, first_ref, second_ref, third_ref, x_ref, tag_ref, total = refs[-7:]
    width = gate_ref.shape[0]
    hidden = gate_ref.shape[1]
    count = blocks[0].shape[0]
    slots = count * len(blocks)
    me = lax.axis_index("dp")
    upper = lax.rem(lax.axis_index("expert"), 2)
    expert = (lax.axis_index("expert") // 2).astype(F32)
    x = jnp.concatenate([block[:, :width] for block in blocks], axis=0).astype(BF16)
    dy = jnp.concatenate([block[:, width : 2 * width] for block in blocks], axis=0).astype(BF16)
    x_ref[...] = x
    total[:, :hidden] = dot_plain(x, gate_ref[...])
    total[:, hidden : 2 * hidden] = dot_plain(x, up_ref[...])
    total[:, 2 * hidden : 3 * hidden] = product_trailing(dy, down_ref[...])
    mine = product_trailing(x, mine_ref[...])
    other = product_trailing(x, other_ref[...])
    low = jnp.where(upper == 1, other, mine)
    high = jnp.where(upper == 1, mine, other)
    total[:, 3 * hidden :] = jnp.concatenate([low, high], axis=1)
    eye = (
        lax.broadcasted_iota(jnp.int32, (count, 128), 0)
        == lax.broadcasted_iota(jnp.int32, (count, 128), 1)
    ).astype(BF16)
    tags = jnp.concatenate(
        [product_leading(block[:, 2 * width :].astype(BF16), eye)[:count] for block in blocks],
        axis=0,
    )
    prob = jnp.zeros((slots, 1), F32)
    for k in range(topk):
        prob += jnp.where(tags[:, k : k + 1] == expert, tags[:, topk + k : topk + k + 1], 0.0)
    lane = lax.broadcasted_iota(jnp.int32, (slots, 128), 1)
    tenant = tags[:, 2 * topk : 2 * topk + 1]
    tag_ref[...] = jnp.where(lane == 0, prob, jnp.where(lane == 1, tenant, 0.0))
    part = slots // 4
    for k, ref in enumerate((own_ref, first_ref, second_ref, third_ref)):
        start = pl.multiple_of((me ^ k) * part, part)
        ref[...] = total[pl.ds(start, part), :].astype(ref.dtype)


def lane_masks(tenant, shape, ranks):
    lane = lax.broadcasted_iota(jnp.int32, shape, 1)
    half = shape[1] // 2
    inner = lax.rem(lane, half)
    is_gate = inner < half // 2
    tenant_of = lax.rem(inner, half // 2) // ranks
    return is_gate, tenant_of.astype(F32) == tenant


def activation_body(ranks, own_ref, first_ref, second_ref, third_ref, tag_ref, maps_ref, out_ref):
    hidden = maps_ref.shape[1]
    part = own_ref.shape[0]
    me = lax.axis_index("dp")
    total = (own_ref[...] + first_ref[...].astype(F32)) + (
        second_ref[...].astype(F32) + third_ref[...].astype(F32)
    )
    tags = tag_ref[pl.ds(pl.multiple_of(me * part, part), part), :]
    prob = tags[:, :1]
    tenant = tags[:, 1:2]
    low = total[:, 3 * hidden :]
    is_gate, keep = lane_masks(tenant, low.shape, ranks)
    low = jnp.where(keep, low, 0.0).astype(BF16)
    low_wide = low.astype(F32)
    maps = maps_ref[...]
    gate = total[:, :hidden] + ADAPTER_SCALE * dot_plain(
        jnp.where(is_gate, low_wide, 0.0).astype(BF16), maps
    )
    up = total[:, hidden : 2 * hidden] + ADAPTER_SCALE * dot_plain(
        jnp.where(is_gate, 0.0, low_wide).astype(BF16), maps
    )
    act = prob * total[:, 2 * hidden : 3 * hidden]
    sig = jax.nn.sigmoid(gate)
    out_ref[:, :hidden] = (act * up * sig * (1.0 + gate * (1.0 - sig))).astype(BF16)
    out_ref[:, hidden : 2 * hidden] = (act * gate * sig).astype(BF16)
    out_ref[:, 2 * hidden :] = low


def backward_body(
    ranks,
    own_ref,
    first_ref,
    second_ref,
    third_ref,
    gate_ref,
    up_ref,
    mine_ref,
    other_ref,
    maps_ref,
    tag_ref,
    keep_ref,
    give_ref,
    back_keep_ref,
    back_give_ref,
    rows_ref,
):
    part = own_ref.shape[0]
    slots = 4 * part
    hidden = gate_ref.shape[1]
    me = lax.axis_index("dp")
    upper = lax.rem(lax.axis_index("expert"), 2)
    for k, ref in enumerate((own_ref, first_ref, second_ref, third_ref)):
        rows_ref[pl.ds(pl.multiple_of((me ^ k) * part, part), part), :] = ref[...]
    gate_grad = rows_ref[:, :hidden]
    up_grad = rows_ref[:, hidden : 2 * hidden]
    maps = maps_ref[...]
    back_gate = product_trailing(gate_grad, maps)
    back_up = product_trailing(up_grad, maps)
    is_gate, keep = lane_masks(tag_ref[:, 1:2], back_gate.shape, ranks)
    back = ADAPTER_SCALE * jnp.where(keep, jnp.where(is_gate, back_gate, back_up), 0.0)
    half = back.shape[1] // 2
    low, high = back[:, :half], back[:, half:]
    mine = jnp.where(upper == 1, high, low)
    other = jnp.where(upper == 1, low, high)
    back_keep_ref[...] = mine
    back_give_ref[...] = other
    total = product_trailing(gate_grad, gate_ref[...])
    total += product_trailing(up_grad, up_ref[...])
    total += dot_plain(mine.astype(BF16), mine_ref[...])
    total += dot_plain(other.astype(BF16), other_ref[...])
    keep_ref[...] = total[: slots // 2]
    give_ref[...] = total[slots // 2 :].astype(BF16)


def join_body(keep_ref, taken_ref, own_ref, first_ref, second_ref, third_ref):
    count = own_ref.shape[0]
    total = keep_ref[...] + taken_ref[...].astype(F32)
    for k, ref in enumerate((own_ref, first_ref, second_ref, third_ref)):
        ref[...] = total[k * count : (k + 1) * count].astype(ref.dtype)


def finish_body(own_ref, first_ref, second_ref, third_ref, out_ref):
    total = (own_ref[...] + first_ref[...].astype(F32)) + (
        second_ref[...].astype(F32) + third_ref[...].astype(F32)
    )
    out_ref[...] = total.astype(BF16)


def maps_grad_body(rows_ref, out_ref):
    hidden = out_ref.shape[1]
    lanes = out_ref.shape[0]
    half = lanes // 2
    row = lax.broadcasted_iota(jnp.int32, (lanes, lanes), 0)
    col = lax.broadcasted_iota(jnp.int32, (lanes, lanes), 1)
    low = rows_ref[:, 2 * hidden :]
    source = lax.rem(col // 8, 2) * half + (col // 16) * 8 + lax.rem(col, 8)
    order = (row == source).astype(BF16)
    low = dot_plain(low, order).astype(BF16)
    out_ref[:half] = ADAPTER_SCALE * product_leading(low[:, :half], rows_ref[:, :hidden])
    out_ref[half:] = ADAPTER_SCALE * product_leading(
        low[:, half:], rows_ref[:, hidden : 2 * hidden]
    )


def input_maps_grad_body(keep_ref, taken_ref, x_ref, out_ref):
    half = keep_ref.shape[0] // 2
    taken = jnp.concatenate([taken_ref[half:], taken_ref[:half]], axis=0)
    back = (keep_ref[...] + taken).astype(BF16)
    out_ref[...] = product_leading(back, x_ref[...])


def dense_shards(
    tokens,
    output_gradient,
    routes,
    router_expert_weight,
    tenant,
    gate_weight,
    up_weight,
    down_weight,
    adapter_input_maps,
    adapter_output_maps,
):
    devices = lax.axis_size("expert")
    chips = devices // 2
    count, width = tokens.shape
    topk = routes.shape[1]
    tenants, rank, hidden = adapter_output_maps.shape[2:]
    ranks = rank // 2
    lanes = 2 * tenants * rank
    slots = devices * count
    part = slots // 4
    mine_cols = adapter_input_maps[0].transpose(1, 2, 3, 0).reshape(lanes // 2, width)
    maps = (
        adapter_output_maps[0]
        .reshape(2, tenants, 2, ranks, hidden)
        .transpose(2, 0, 1, 3, 4)
        .reshape(lanes, hidden)
    )
    other_cols = swap(mine_cols, "expert", 1)
    (packed,) = local_call(
        pack_body,
        [((count, 2 * width + 128), BF16)],
        (tokens, output_gradient, routes.T, router_expert_weight.T, tenant[None, :]),
    )
    same_core = [packed] + [swap(packed, "expert", 2 * k) for k in range(1, chips)]
    other_core = [swap(block, "expert", 1) for block in same_core]
    gate, up, down = gate_weight[0], up_weight[0], down_weight[0]
    columns = 3 * hidden + lanes
    own, first, second, third, x, tags = local_call(
        functools.partial(forward_body, topk),
        [
            ((part, columns), F32),
            ((part, columns), BF16),
            ((part, columns), BF16),
            ((part, columns), BF16),
            ((slots, width), BF16),
            ((slots, 128), F32),
        ],
        (*same_core, *other_core, gate, up, down, mine_cols, other_cols),
        scratch=[pltpu.VMEM((slots, columns), F32)],
        flops=2 * slots * width * columns,
        moved=4 * width * columns,
    )
    sums = [own] + [swap(block, "dp", k + 1) for k, block in enumerate((first, second, third))]
    (gradients,) = local_call(
        functools.partial(activation_body, ranks),
        [((part, 2 * hidden + lanes), BF16)],
        (*sums, tags, maps),
    )
    gathered = [gradients] + [swap(gradients, "dp", k) for k in (1, 2, 3)]
    keep, give, back_keep, back_give, rows = local_call(
        functools.partial(backward_body, ranks),
        [
            ((slots // 2, width), F32),
            ((slots // 2, width), BF16),
            ((slots, lanes // 2), F32),
            ((slots, lanes // 2), F32),
            ((slots, 2 * hidden + lanes), BF16),
        ],
        (*gathered, gate, up, mine_cols, other_cols, maps, tags),
        flops=4 * slots * width * hidden,
        moved=4 * width * hidden,
    )
    taken = swap(give, "expert", 1)
    back_taken = swap(back_give, "expert", 1)
    own, first, second, third = local_call(
        join_body,
        [((count, width), F32)] + [((count, width), BF16)] * 3,
        (keep, taken),
    )
    returned = [own] + [
        swap(block, "expert", 2 * (k + 1)) for k, block in enumerate((first, second, third))
    ]
    (maps_grad,) = local_call(maps_grad_body, [((lanes, hidden), F32)], (rows,))
    (input_maps_grad,) = local_call(
        input_maps_grad_body, [((lanes // 2, width), F32)], (back_keep, back_taken, x)
    )
    (input_grad,) = local_call(finish_body, [((count, width), BF16)], returned)
    adapter_a_grad = (
        input_maps_grad.reshape(2, tenants, ranks, width).transpose(3, 0, 1, 2)[None]
    )
    adapter_b_grad = maps_grad.reshape(1, 2, tenants, rank, hidden)
    return input_grad, adapter_a_grad, adapter_b_grad


def shards(*arrays):
    tokens, routes, maps = arrays[0], arrays[2], arrays[9]
    devices = lax.axis_size("expert")
    capacity = 4 * tokens.shape[0] * routes.shape[1] // devices
    if (
        capacity >= tokens.shape[0]
        and devices == 8
        and lax.axis_size("dp") == 4
        and tokens.shape[0] == 8
        and maps.shape[2] * maps.shape[3] == 64
    ):
        return dense_shards(*arrays)
    return routed_shards(*arrays)


def solution(mesh):
    placed = (
        P("expert", "dp"),
        P("expert", "dp"),
        P("expert", None),
        P("expert", None),
        P("expert"),
        P("expert", "dp", None),
        P("expert", "dp", None),
        P("expert", None, "dp"),
        P("expert", "dp", None, None, None),
        P("expert", None, None, None, None),
    )
    return jax.shard_map(
        shards,
        mesh=mesh,
        in_specs=placed,
        out_specs=(
            P("expert", "dp"),
            P("expert", "dp", None, None, None),
            P("expert", None, None, None, None),
        ),
        check_vma=False,
    )
```

```python
import functools

import jax
import jax.numpy as jnp
from jax import lax
from jax.experimental import pallas as pl
from jax.experimental.pallas import tpu as pltpu
from jax.sharding import PartitionSpec as P

ADAPTER_SCALE = 2.0


def partner(shard, axis, bit):
    return lax.ppermute(shard, axis, [(i, i ^ 1 << bit) for i in range(lax.axis_size(axis))])


def product_leading(left, right):
    return lax.dot_general(
        left, right, (((0,), (0,)), ((), ())), preferred_element_type=jnp.float32
    )


def product_trailing(left, right):
    return lax.dot_general(
        left, right, (((1,), (1,)), ((), ())), preferred_element_type=jnp.float32
    )


def order_halves(mine, other, upper):
    return (jnp.where(upper, other, mine), jnp.where(upper, mine, other))


def spread(values, tenant_mask, tenant_list, adapter_rank_width):
    count = values.shape[0]
    wide = tenant_mask[:, None, :, None] * values.astype(jnp.float32).reshape(
        count, 2, 1, adapter_rank_width
    )
    return wide.reshape(count, 2, tenant_list * adapter_rank_width).astype(jnp.bfloat16)


def routed_shards(
    tokens,
    output_gradient,
    routes,
    router_expert_weight,
    tenant,
    gate_weight,
    up_weight,
    down_weight,
    adapter_input_maps,
    adapter_output_maps,
):
    devices = lax.axis_size("expert")
    experts = devices // 2
    tok_col, quarter = tokens.shape
    topk = routes.shape[1]
    tenant_list = adapter_output_maps.shape[2]
    adapter_rank_width = adapter_output_maps.shape[3]
    hidden_halfway = adapter_output_maps.shape[4]
    rank_halfway = adapter_rank_width // 2
    capacity = 2 * tok_col * topk // experts
    half_cap = capacity // 2
    slots = devices * capacity
    upper = lax.axis_index("expert") % 2 == 1
    flat_route = routes.reshape(-1)
    expert_hot = (flat_route[:, None] == jnp.arange(experts, dtype=jnp.int32)[None, :]).astype(
        jnp.int32
    )
    earlier = jnp.cumsum(expert_hot, axis=0) - expert_hot
    position = jnp.sum(earlier * expert_hot, axis=1)
    slot_of = (flat_route * capacity + position).reshape(tok_col, topk)
    slot_range = jnp.arange(experts * capacity, dtype=jnp.int32)
    hits = (slot_range[:, None, None] == slot_of[None, :, :]).astype(jnp.float32)
    select_tok = jnp.sum(hits, axis=2)
    prob_tok = jnp.sum(hits * router_expert_weight.astype(jnp.float32)[None, :, :], axis=2)
    tenant_hot = (tenant[:, None] == jnp.arange(tenant_list, dtype=jnp.int32)[None, :]).astype(
        jnp.float32
    )
    select_bf = select_tok.astype(jnp.bfloat16)
    send_rows = jnp.dot(select_bf, tokens, preferred_element_type=jnp.float32).astype(jnp.bfloat16)
    send_grad = jnp.dot(select_bf, output_gradient, preferred_element_type=jnp.float32).astype(
        jnp.bfloat16
    )
    send_tag = jnp.dot(prob_tok, tenant_hot, precision=lax.Precision.HIGHEST).astype(jnp.bfloat16)

    def doubled(block):
        wide = block.reshape(experts, 1, capacity, block.shape[1])
        return jnp.broadcast_to(wide, (experts, 2, capacity, block.shape[1])).reshape(
            devices, capacity, block.shape[1]
        )

    got_rows, got_grad, got_tag = (
        lax.all_to_all(doubled(send_rows), "expert", split_axis=0, concat_axis=0, tiled=True),
        lax.all_to_all(doubled(send_grad), "expert", split_axis=0, concat_axis=0, tiled=True),
        lax.all_to_all(doubled(send_tag), "expert", split_axis=0, concat_axis=0, tiled=True),
    )
    input_rows = got_rows.reshape(slots, quarter)
    rows_dy = got_grad.reshape(slots, quarter)
    tags = got_tag.reshape(slots, tenant_list).astype(jnp.float32)
    tenant_mask = (tags > 0).astype(jnp.float32)
    slot_prob = jnp.sum(tags, axis=1)
    adapter_local = adapter_input_maps[0]
    adapter_other = partner(adapter_local, "expert", 0)
    low_rank, high_rank = order_halves(adapter_local, adapter_other, upper)
    adapter_cols = jnp.concatenate([low_rank, high_rank], axis=-1).reshape(
        quarter, 2 * tenant_list * adapter_rank_width
    )
    gate_output_map = adapter_output_maps[0, 0].reshape(
        tenant_list * adapter_rank_width, hidden_halfway
    )
    up_output_map = adapter_output_maps[0, 1].reshape(
        tenant_list * adapter_rank_width, hidden_halfway
    )
    gate_part = jnp.dot(input_rows, gate_weight[0], preferred_element_type=jnp.float32)
    up_part = jnp.dot(input_rows, up_weight[0], preferred_element_type=jnp.float32)
    act_part = product_trailing(rows_dy, down_weight[0])
    proj_all = jnp.dot(input_rows, adapter_cols, preferred_element_type=jnp.float32).reshape(
        slots, 2, tenant_list, adapter_rank_width
    )
    proj_part = jnp.sum(proj_all * tenant_mask[:, None, :, None], axis=2).reshape(
        slots, 2 * adapter_rank_width
    )
    gate_total, up_total, act_sum, proj_sum = lax.psum(
        (gate_part, up_part, act_part, proj_part), "dp"
    )
    proj_low = proj_sum.astype(jnp.bfloat16)
    spread_in = spread(proj_low, tenant_mask, tenant_list, adapter_rank_width)
    gate_preactivation = gate_total + ADAPTER_SCALE * jnp.dot(
        spread_in[:, 0], gate_output_map, preferred_element_type=jnp.float32
    )
    up_preactivation = up_total + ADAPTER_SCALE * jnp.dot(
        spread_in[:, 1], up_output_map, preferred_element_type=jnp.float32
    )
    act_grad = slot_prob[:, None] * act_sum
    gate_sig = jax.nn.sigmoid(gate_preactivation)
    gate_gradient = (
        act_grad * up_preactivation * gate_sig * (1.0 + gate_preactivation * (1.0 - gate_sig))
    ).astype(jnp.bfloat16)
    up_gradient = (act_grad * gate_preactivation * gate_sig).astype(jnp.bfloat16)
    gate_gradient, up_gradient, proj_low = (gate_gradient, up_gradient, proj_low)
    projection_spread = spread(proj_low, tenant_mask, tenant_list, adapter_rank_width)
    gate_output_map_gradient = ADAPTER_SCALE * product_leading(
        projection_spread[:, 0], gate_gradient
    )
    up_output_map_gradient = ADAPTER_SCALE * product_leading(projection_spread[:, 1], up_gradient)
    adapter_b_grad = jnp.stack([gate_output_map_gradient, up_output_map_gradient]).reshape(
        1, 2, tenant_list, adapter_rank_width, hidden_halfway
    )
    backward_total = ADAPTER_SCALE * jnp.stack(
        [
            product_trailing(gate_gradient, gate_output_map),
            product_trailing(up_gradient, up_output_map),
        ],
        axis=1,
    )
    back_part = jnp.sum(
        backward_total.reshape(slots, 2, tenant_list, adapter_rank_width)
        * tenant_mask[:, None, :, None],
        axis=2,
    ).reshape(slots, 2 * adapter_rank_width)
    input_part = product_trailing(gate_gradient, gate_weight[0]) + product_trailing(
        up_gradient, up_weight[0]
    )
    by_source = input_part.reshape(devices, capacity, quarter)
    first_half = by_source[:, :half_cap]
    second_half = by_source[:, half_cap:]
    keep_half = jnp.where(upper, second_half, first_half)
    give_half = jnp.where(upper, first_half, second_half)
    taken_half, back_other = partner((give_half, back_part), "expert", 0)
    input_half = keep_half + taken_half
    back_low = (back_part + back_other).astype(jnp.bfloat16)
    back_spread = spread(back_low, tenant_mask, tenant_list, adapter_rank_width)
    spread_rows = back_spread.reshape(devices, capacity, 2 * tenant_list * adapter_rank_width)
    spread_half = jnp.where(upper, spread_rows[:, half_cap:], spread_rows[:, :half_cap]).reshape(
        devices * half_cap, 2 * tenant_list * adapter_rank_width
    )
    adapter_term = product_trailing(spread_half, adapter_cols).reshape(devices, half_cap, quarter)
    slot_grad = (input_half + adapter_term).astype(jnp.bfloat16)
    spread_ranks = back_spread.reshape(slots, 2, tenant_list, adapter_rank_width)
    mine_cols = jnp.where(
        upper, spread_ranks[..., rank_halfway:], spread_ranks[..., :rank_halfway]
    ).reshape(slots, 2 * tenant_list * rank_halfway)
    adapter_a_grad = product_leading(input_rows, mine_cols).reshape(
        1, quarter, 2, tenant_list, rank_halfway
    )
    returned = lax.all_to_all(slot_grad, "expert", split_axis=0, concat_axis=0, tiled=True)
    slot_rows = returned.reshape(experts * capacity, quarter)
    input_grad = product_leading(select_bf, slot_rows).astype(jnp.bfloat16)
    return (input_grad, adapter_a_grad, adapter_b_grad)


F32 = jnp.float32
BF16 = jnp.bfloat16
VMEM = pl.BlockSpec(memory_space=pltpu.VMEM)
HBM = pl.BlockSpec(memory_space=pltpu.HBM)


def local_call(body, outs, operands, scratch=(), flops=0, moved=0, far=0):
    operands = [
        pltpu.with_memory_space_constraint(array, pltpu.HBM) if k < far else array
        for k, array in enumerate(operands)
    ]
    return pl.pallas_call(
        body,
        out_shape=[jax.ShapeDtypeStruct(shape, kind) for shape, kind in outs],
        in_specs=[HBM] * far + [VMEM] * (len(operands) - far),
        out_specs=[VMEM] * len(outs),
        scratch_shapes=list(scratch),
        cost_estimate=pl.CostEstimate(flops=flops, bytes_accessed=moved, transcendentals=0),
        compiler_params=pltpu.CompilerParams(vmem_limit_bytes=16 << 20),
    )(*operands)


def dot_plain(left, right):
    return lax.dot_general(left, right, (((1,), (0,)), ((), ())), preferred_element_type=F32)


def swap(array, axis, offset):
    return lax.ppermute(array, axis, [(i, i ^ offset) for i in range(lax.axis_size(axis))])


def pack_body(
    x_ref, dy_ref, routes_ref, weight_ref, tenant_ref, out_ref, routes, weight, tenant, arrived
):
    width = x_ref.shape[1]
    topk, count = routes_ref.shape
    copies = [
        pltpu.make_async_copy(source, target, arrived.at[k])
        for k, (source, target) in enumerate(
            (
                (routes_ref, routes),
                (weight_ref, weight),
                (tenant_ref, tenant),
                (x_ref, out_ref.at[:, :width]),
                (dy_ref, out_ref.at[:, width : 2 * width]),
            )
        )
    ]
    for copy in copies:
        copy.start()
    for copy in copies[:3]:
        copy.wait()
    tags = [routes[...].astype(F32), weight[...].astype(F32), tenant[...].astype(F32)]
    rows = 2 * topk + 1
    tags = jnp.concatenate(tags + [jnp.zeros((count - rows, count), F32)], axis=0)
    tags = jnp.concatenate([tags, jnp.zeros((count, 128 - count), F32)], axis=1)
    out_ref[:, 2 * width :] = tags.astype(BF16)
    for copy in copies[3:]:
        copy.wait()


def stage_body(*refs):
    count = (len(refs) - 2) // 2
    sources, targets, maps, arrived = refs[:count], refs[count : 2 * count], refs[-2], refs[-1]
    copies = [
        pltpu.make_async_copy(source, target, arrived.at[k])
        for k, (source, target) in enumerate(zip(sources, targets[:-1] + (maps,)))
    ]
    for copy in copies:
        copy.start()
    copies[-1].wait()
    targets[-1][...] = dot_plain(rank_order(maps.shape[0], False), maps[...]).astype(BF16)
    for copy in copies[:-1]:
        copy.wait()


def rank_order(lanes, columns):
    at = lax.broadcasted_iota(jnp.int32, (lanes, lanes), 0 if columns else 1)
    place = lax.broadcasted_iota(jnp.int32, (lanes, lanes), 1 if columns else 0)
    if not columns:
        at, place = place, at
    source = lax.rem(place // 8, 2) * (lanes // 2) + (place // 16) * 8 + lax.rem(place, 8)
    return (at == source).astype(BF16)


def forward_body(topk, *refs):
    blocks = [ref[...].astype(F32) for ref in refs[:-12]]
    gate_ref, up_ref, down_ref, mine_ref, other_ref = refs[-12:-7]
    own_ref, first_ref, second_ref, third_ref, x_ref, tag_ref, total = refs[-7:]
    width = gate_ref.shape[0]
    hidden = gate_ref.shape[1]
    count = blocks[0].shape[0]
    slots = count * len(blocks)
    me = lax.axis_index("dp")
    upper = lax.rem(lax.axis_index("expert"), 2)
    expert = (lax.axis_index("expert") // 2).astype(F32)
    x = jnp.concatenate([block[:, :width] for block in blocks], axis=0).astype(BF16)
    dy = jnp.concatenate([block[:, width : 2 * width] for block in blocks], axis=0).astype(BF16)
    x_ref[...] = x
    total[:, :hidden] = dot_plain(x, gate_ref[...])
    total[:, hidden : 2 * hidden] = dot_plain(x, up_ref[...])
    total[:, 2 * hidden : 3 * hidden] = product_trailing(dy, down_ref[...])
    mine = product_trailing(x, mine_ref[...])
    other = product_trailing(x, other_ref[...])
    low = jnp.where(upper == 1, other, mine)
    high = jnp.where(upper == 1, mine, other)
    total[:, 3 * hidden :] = jnp.concatenate([low, high], axis=1)
    eye = (
        lax.broadcasted_iota(jnp.int32, (count, 128), 0)
        == lax.broadcasted_iota(jnp.int32, (count, 128), 1)
    ).astype(BF16)
    tags = jnp.concatenate(
        [product_leading(block[:, 2 * width :].astype(BF16), eye)[:count] for block in blocks],
        axis=0,
    )
    prob = jnp.zeros((slots, 1), F32)
    for k in range(topk):
        prob += jnp.where(tags[:, k : k + 1] == expert, tags[:, topk + k : topk + k + 1], 0.0)
    lane = lax.broadcasted_iota(jnp.int32, (slots, 128), 1)
    tenant = tags[:, 2 * topk : 2 * topk + 1]
    tag_ref[...] = jnp.where(lane == 0, prob, jnp.where(lane == 1, tenant, 0.0))
    part = slots // 4
    for k, ref in enumerate((own_ref, first_ref, second_ref, third_ref)):
        start = pl.multiple_of((me ^ k) * part, part)
        ref[...] = total[pl.ds(start, part), :].astype(ref.dtype)


def lane_masks(tenant, shape, ranks):
    lane = lax.broadcasted_iota(jnp.int32, shape, 1)
    half = shape[1] // 2
    inner = lax.rem(lane, half)
    is_gate = inner < half // 2
    tenant_of = lax.rem(inner, half // 2) // ranks
    return is_gate, tenant_of.astype(F32) == tenant


def activation_body(ranks, own_ref, third_ref, second_ref, first_ref, tag_ref, maps_ref, out_ref):
    hidden = maps_ref.shape[1]
    part = own_ref.shape[0]
    me = lax.axis_index("dp")
    total = (own_ref[...] + first_ref[...].astype(F32)) + (
        second_ref[...].astype(F32) + third_ref[...].astype(F32)
    )
    tags = tag_ref[pl.ds(pl.multiple_of(me * part, part), part), :]
    prob = tags[:, :1]
    tenant = tags[:, 1:2]
    low = total[:, 3 * hidden :]
    is_gate, keep = lane_masks(tenant, low.shape, ranks)
    low = jnp.where(keep, low, 0.0).astype(BF16)
    low_wide = low.astype(F32)
    maps = maps_ref[...]
    gate = total[:, :hidden] + ADAPTER_SCALE * dot_plain(
        jnp.where(is_gate, low_wide, 0.0).astype(BF16), maps
    )
    up = total[:, hidden : 2 * hidden] + ADAPTER_SCALE * dot_plain(
        jnp.where(is_gate, 0.0, low_wide).astype(BF16), maps
    )
    act = prob * total[:, 2 * hidden : 3 * hidden]
    sig = jax.nn.sigmoid(gate)
    out_ref[:, :hidden] = (act * up * sig * (1.0 + gate * (1.0 - sig))).astype(BF16)
    out_ref[:, hidden : 2 * hidden] = (act * gate * sig).astype(BF16)
    out_ref[:, 2 * hidden :] = low


def backward_body(
    ranks,
    own_ref,
    first_ref,
    second_ref,
    third_ref,
    gate_ref,
    up_ref,
    mine_ref,
    other_ref,
    maps_ref,
    tag_ref,
    keep_ref,
    give_ref,
    back_keep_ref,
    back_give_ref,
    rows_ref,
):
    part = own_ref.shape[0]
    slots = 4 * part
    hidden = gate_ref.shape[1]
    me = lax.axis_index("dp")
    upper = lax.rem(lax.axis_index("expert"), 2)
    for k, ref in enumerate((own_ref, first_ref, second_ref, third_ref)):
        rows_ref[pl.ds(pl.multiple_of((me ^ k) * part, part), part), :] = ref[...]
    gate_grad = rows_ref[:, :hidden]
    up_grad = rows_ref[:, hidden : 2 * hidden]
    maps = maps_ref[...]
    back_gate = product_trailing(gate_grad, maps)
    back_up = product_trailing(up_grad, maps)
    is_gate, keep = lane_masks(tag_ref[:, 1:2], back_gate.shape, ranks)
    back = ADAPTER_SCALE * jnp.where(keep, jnp.where(is_gate, back_gate, back_up), 0.0)
    half = back.shape[1] // 2
    low, high = back[:, :half], back[:, half:]
    mine = jnp.where(upper == 1, high, low)
    other = jnp.where(upper == 1, low, high)
    back_keep_ref[...] = mine
    back_give_ref[...] = other
    total = product_trailing(gate_grad, gate_ref[...])
    total += product_trailing(up_grad, up_ref[...])
    total += dot_plain(mine.astype(BF16), mine_ref[...])
    total += dot_plain(other.astype(BF16), other_ref[...])
    keep_ref[...] = total[: slots // 2]
    give_ref[...] = total[slots // 2 :].astype(BF16)


def join_body(keep_ref, taken_ref, own_ref, first_ref, second_ref, third_ref):
    count = own_ref.shape[0]
    total = keep_ref[...] + taken_ref[...].astype(F32)
    for k, ref in enumerate((own_ref, first_ref, second_ref, third_ref)):
        ref[...] = total[k * count : (k + 1) * count].astype(ref.dtype)


def finish_body(own_ref, third_ref, second_ref, first_ref, out_ref):
    total = (own_ref[...] + first_ref[...].astype(F32)) + (
        second_ref[...].astype(F32) + third_ref[...].astype(F32)
    )
    out_ref[...] = total.astype(BF16)


def maps_grad_body(rows_ref, out_ref):
    hidden = out_ref.shape[1]
    lanes = out_ref.shape[0]
    half = lanes // 2
    low = dot_plain(rows_ref[:, 2 * hidden :], rank_order(lanes, True)).astype(BF16)
    out_ref[:half] = ADAPTER_SCALE * product_leading(low[:, :half], rows_ref[:, :hidden])
    out_ref[half:] = ADAPTER_SCALE * product_leading(
        low[:, half:], rows_ref[:, hidden : 2 * hidden]
    )


def input_maps_grad_body(keep_ref, taken_ref, x_ref, out_ref):
    half = keep_ref.shape[0] // 2
    taken = jnp.concatenate([taken_ref[half:], taken_ref[:half]], axis=0)
    back = (keep_ref[...] + taken).astype(BF16)
    out_ref[...] = product_leading(back, x_ref[...])


def dense_shards(
    tokens,
    output_gradient,
    routes,
    router_expert_weight,
    tenant,
    gate_weight,
    up_weight,
    down_weight,
    adapter_input_maps,
    adapter_output_maps,
):
    devices = lax.axis_size("expert")
    chips = devices // 2
    count, width = tokens.shape
    topk = routes.shape[1]
    tenants, rank, hidden = adapter_output_maps.shape[2:]
    ranks = rank // 2
    lanes = 2 * tenants * rank
    slots = devices * count
    part = slots // 4
    mine_cols = adapter_input_maps[0].transpose(1, 2, 3, 0).reshape(lanes // 2, width)
    other_cols = swap(mine_cols, "expert", 1)
    (packed,) = local_call(
        pack_body,
        [((count, 2 * width + 128), BF16)],
        (tokens, output_gradient, routes.T, router_expert_weight.T, tenant[None, :]),
        scratch=[
            pltpu.VMEM((topk, count), jnp.int32),
            pltpu.VMEM((topk, count), BF16),
            pltpu.VMEM((1, count), jnp.int32),
            pltpu.SemaphoreType.DMA((5,)),
        ],
        far=5,
    )
    stored = (
        gate_weight[0],
        up_weight[0],
        down_weight[0],
        mine_cols,
        adapter_output_maps.reshape(lanes, hidden),
    )
    gate, up, down, mine_cols, maps = local_call(
        stage_body,
        [(array.shape, BF16) for array in stored],
        stored,
        scratch=[pltpu.VMEM((lanes, hidden), BF16), pltpu.SemaphoreType.DMA((len(stored),))],
        moved=sum(2 * array.size for array in stored),
        far=len(stored),
    )
    same_core = [packed] + [swap(packed, "expert", 2 * k) for k in range(1, chips)]
    same_core[-1], (gate, up, down, mine_cols, maps) = lax.optimization_barrier(
        (same_core[-1], (gate, up, down, mine_cols, maps))
    )
    other_core = [swap(block, "expert", 1) for block in same_core]
    columns = 3 * hidden + lanes
    own, first, second, third, x, tags = local_call(
        functools.partial(forward_body, topk),
        [
            ((part, columns), F32),
            ((part, columns), BF16),
            ((part, columns), BF16),
            ((part, columns), BF16),
            ((slots, width), BF16),
            ((slots, 128), F32),
        ],
        (*same_core, *other_core, gate, up, down, mine_cols, other_cols),
        scratch=[pltpu.VMEM((slots, columns), F32)],
        flops=2 * slots * width * columns,
        moved=4 * width * columns,
    )
    third, second, first = swap(third, "dp", 3), swap(second, "dp", 2), swap(first, "dp", 1)
    sums = [own, third, second, first]
    (gradients,) = local_call(
        functools.partial(activation_body, ranks),
        [((part, 2 * hidden + lanes), BF16)],
        (*sums, tags, maps),
    )
    gathered = [gradients] + [swap(gradients, "dp", k) for k in (1, 2, 3)]
    keep, give, back_keep, back_give, rows = local_call(
        functools.partial(backward_body, ranks),
        [
            ((slots // 2, width), F32),
            ((slots // 2, width), BF16),
            ((slots, lanes // 2), F32),
            ((slots, lanes // 2), F32),
            ((slots, 2 * hidden + lanes), BF16),
        ],
        (*gathered, gate, up, mine_cols, other_cols, maps, tags),
        flops=4 * slots * width * hidden,
        moved=4 * width * hidden,
    )
    taken = swap(give, "expert", 1)
    back_taken = swap(back_give, "expert", 1)
    own, first, second, third = local_call(
        join_body,
        [((count, width), F32)] + [((count, width), BF16)] * 3,
        (keep, taken),
    )
    third, second = swap(third, "expert", 6), swap(second, "expert", 4)
    returned = [own, third, second, swap(first, "expert", 2)]
    (maps_grad,) = local_call(maps_grad_body, [((lanes, hidden), F32)], (rows,))
    (input_maps_grad,) = local_call(
        input_maps_grad_body, [((lanes // 2, width), F32)], (back_keep, back_taken, x)
    )
    (input_grad,) = local_call(finish_body, [((count, width), BF16)], returned)
    adapter_a_grad = (
        input_maps_grad.reshape(2, tenants, ranks, width).transpose(3, 0, 1, 2)[None]
    )
    adapter_b_grad = maps_grad.reshape(1, 2, tenants, rank, hidden)
    return input_grad, adapter_a_grad, adapter_b_grad


def shards(*arrays):
    tokens, routes, maps = arrays[0], arrays[2], arrays[9]
    devices = lax.axis_size("expert")
    capacity = 4 * tokens.shape[0] * routes.shape[1] // devices
    if (
        capacity >= tokens.shape[0]
        and devices == 8
        and lax.axis_size("dp") == 4
        and tokens.shape[0] == 8
        and maps.shape[2] * maps.shape[3] == 64
    ):
        return dense_shards(*arrays)
    return routed_shards(*arrays)


def solution(mesh):
    placed = (
        P("expert", "dp"),
        P("expert", "dp"),
        P("expert", None),
        P("expert", None),
        P("expert"),
        P("expert", "dp", None),
        P("expert", "dp", None),
        P("expert", None, "dp"),
        P("expert", "dp", None, None, None),
        P("expert", None, None, None, None),
    )
    return jax.shard_map(
        shards,
        mesh=mesh,
        in_specs=placed,
        out_specs=(
            P("expert", "dp"),
            P("expert", "dp", None, None, None),
            P("expert", None, None, None, None),
        ),
        check_vma=False,
    )
```

```python
import functools

import jax
import jax.numpy as jnp
from jax import lax
from jax.experimental import pallas as pl
from jax.experimental.pallas import tpu as pltpu
from jax.sharding import PartitionSpec as P

ADAPTER_SCALE = 2.0


def partner(shard, axis, bit):
    return lax.ppermute(shard, axis, [(i, i ^ 1 << bit) for i in range(lax.axis_size(axis))])


def product_leading(left, right):
    return lax.dot_general(
        left, right, (((0,), (0,)), ((), ())), preferred_element_type=jnp.float32
    )


def product_trailing(left, right):
    return lax.dot_general(
        left, right, (((1,), (1,)), ((), ())), preferred_element_type=jnp.float32
    )


def order_halves(mine, other, upper):
    return (jnp.where(upper, other, mine), jnp.where(upper, mine, other))


def spread(values, tenant_mask, tenant_list, adapter_rank_width):
    count = values.shape[0]
    wide = tenant_mask[:, None, :, None] * values.astype(jnp.float32).reshape(
        count, 2, 1, adapter_rank_width
    )
    return wide.reshape(count, 2, tenant_list * adapter_rank_width).astype(jnp.bfloat16)


def routed_shards(
    tokens,
    output_gradient,
    routes,
    router_expert_weight,
    tenant,
    gate_weight,
    up_weight,
    down_weight,
    adapter_input_maps,
    adapter_output_maps,
):
    devices = lax.axis_size("expert")
    experts = devices // 2
    tok_col, quarter = tokens.shape
    topk = routes.shape[1]
    tenant_list = adapter_output_maps.shape[2]
    adapter_rank_width = adapter_output_maps.shape[3]
    hidden_halfway = adapter_output_maps.shape[4]
    rank_halfway = adapter_rank_width // 2
    capacity = 2 * tok_col * topk // experts
    half_cap = capacity // 2
    slots = devices * capacity
    upper = lax.axis_index("expert") % 2 == 1
    flat_route = routes.reshape(-1)
    expert_hot = (flat_route[:, None] == jnp.arange(experts, dtype=jnp.int32)[None, :]).astype(
        jnp.int32
    )
    earlier = jnp.cumsum(expert_hot, axis=0) - expert_hot
    position = jnp.sum(earlier * expert_hot, axis=1)
    slot_of = (flat_route * capacity + position).reshape(tok_col, topk)
    slot_range = jnp.arange(experts * capacity, dtype=jnp.int32)
    hits = (slot_range[:, None, None] == slot_of[None, :, :]).astype(jnp.float32)
    select_tok = jnp.sum(hits, axis=2)
    prob_tok = jnp.sum(hits * router_expert_weight.astype(jnp.float32)[None, :, :], axis=2)
    tenant_hot = (tenant[:, None] == jnp.arange(tenant_list, dtype=jnp.int32)[None, :]).astype(
        jnp.float32
    )
    select_bf = select_tok.astype(jnp.bfloat16)
    send_rows = jnp.dot(select_bf, tokens, preferred_element_type=jnp.float32).astype(jnp.bfloat16)
    send_grad = jnp.dot(select_bf, output_gradient, preferred_element_type=jnp.float32).astype(
        jnp.bfloat16
    )
    send_tag = jnp.dot(prob_tok, tenant_hot, precision=lax.Precision.HIGHEST).astype(jnp.bfloat16)

    def doubled(block):
        wide = block.reshape(experts, 1, capacity, block.shape[1])
        return jnp.broadcast_to(wide, (experts, 2, capacity, block.shape[1])).reshape(
            devices, capacity, block.shape[1]
        )

    got_rows, got_grad, got_tag = (
        lax.all_to_all(doubled(send_rows), "expert", split_axis=0, concat_axis=0, tiled=True),
        lax.all_to_all(doubled(send_grad), "expert", split_axis=0, concat_axis=0, tiled=True),
        lax.all_to_all(doubled(send_tag), "expert", split_axis=0, concat_axis=0, tiled=True),
    )
    input_rows = got_rows.reshape(slots, quarter)
    rows_dy = got_grad.reshape(slots, quarter)
    tags = got_tag.reshape(slots, tenant_list).astype(jnp.float32)
    tenant_mask = (tags > 0).astype(jnp.float32)
    slot_prob = jnp.sum(tags, axis=1)
    adapter_local = adapter_input_maps[0]
    adapter_other = partner(adapter_local, "expert", 0)
    low_rank, high_rank = order_halves(adapter_local, adapter_other, upper)
    adapter_cols = jnp.concatenate([low_rank, high_rank], axis=-1).reshape(
        quarter, 2 * tenant_list * adapter_rank_width
    )
    gate_output_map = adapter_output_maps[0, 0].reshape(
        tenant_list * adapter_rank_width, hidden_halfway
    )
    up_output_map = adapter_output_maps[0, 1].reshape(
        tenant_list * adapter_rank_width, hidden_halfway
    )
    gate_part = jnp.dot(input_rows, gate_weight[0], preferred_element_type=jnp.float32)
    up_part = jnp.dot(input_rows, up_weight[0], preferred_element_type=jnp.float32)
    act_part = product_trailing(rows_dy, down_weight[0])
    proj_all = jnp.dot(input_rows, adapter_cols, preferred_element_type=jnp.float32).reshape(
        slots, 2, tenant_list, adapter_rank_width
    )
    proj_part = jnp.sum(proj_all * tenant_mask[:, None, :, None], axis=2).reshape(
        slots, 2 * adapter_rank_width
    )
    gate_total, up_total, act_sum, proj_sum = lax.psum(
        (gate_part, up_part, act_part, proj_part), "dp"
    )
    proj_low = proj_sum.astype(jnp.bfloat16)
    spread_in = spread(proj_low, tenant_mask, tenant_list, adapter_rank_width)
    gate_preactivation = gate_total + ADAPTER_SCALE * jnp.dot(
        spread_in[:, 0], gate_output_map, preferred_element_type=jnp.float32
    )
    up_preactivation = up_total + ADAPTER_SCALE * jnp.dot(
        spread_in[:, 1], up_output_map, preferred_element_type=jnp.float32
    )
    act_grad = slot_prob[:, None] * act_sum
    gate_sig = jax.nn.sigmoid(gate_preactivation)
    gate_gradient = (
        act_grad * up_preactivation * gate_sig * (1.0 + gate_preactivation * (1.0 - gate_sig))
    ).astype(jnp.bfloat16)
    up_gradient = (act_grad * gate_preactivation * gate_sig).astype(jnp.bfloat16)
    gate_gradient, up_gradient, proj_low = (gate_gradient, up_gradient, proj_low)
    projection_spread = spread(proj_low, tenant_mask, tenant_list, adapter_rank_width)
    gate_output_map_gradient = ADAPTER_SCALE * product_leading(
        projection_spread[:, 0], gate_gradient
    )
    up_output_map_gradient = ADAPTER_SCALE * product_leading(projection_spread[:, 1], up_gradient)
    adapter_b_grad = jnp.stack([gate_output_map_gradient, up_output_map_gradient]).reshape(
        1, 2, tenant_list, adapter_rank_width, hidden_halfway
    )
    backward_total = ADAPTER_SCALE * jnp.stack(
        [
            product_trailing(gate_gradient, gate_output_map),
            product_trailing(up_gradient, up_output_map),
        ],
        axis=1,
    )
    back_part = jnp.sum(
        backward_total.reshape(slots, 2, tenant_list, adapter_rank_width)
        * tenant_mask[:, None, :, None],
        axis=2,
    ).reshape(slots, 2 * adapter_rank_width)
    input_part = product_trailing(gate_gradient, gate_weight[0]) + product_trailing(
        up_gradient, up_weight[0]
    )
    by_source = input_part.reshape(devices, capacity, quarter)
    first_half = by_source[:, :half_cap]
    second_half = by_source[:, half_cap:]
    keep_half = jnp.where(upper, second_half, first_half)
    give_half = jnp.where(upper, first_half, second_half)
    taken_half, back_other = partner((give_half, back_part), "expert", 0)
    input_half = keep_half + taken_half
    back_low = (back_part + back_other).astype(jnp.bfloat16)
    back_spread = spread(back_low, tenant_mask, tenant_list, adapter_rank_width)
    spread_rows = back_spread.reshape(devices, capacity, 2 * tenant_list * adapter_rank_width)
    spread_half = jnp.where(upper, spread_rows[:, half_cap:], spread_rows[:, :half_cap]).reshape(
        devices * half_cap, 2 * tenant_list * adapter_rank_width
    )
    adapter_term = product_trailing(spread_half, adapter_cols).reshape(devices, half_cap, quarter)
    slot_grad = (input_half + adapter_term).astype(jnp.bfloat16)
    spread_ranks = back_spread.reshape(slots, 2, tenant_list, adapter_rank_width)
    mine_cols = jnp.where(
        upper, spread_ranks[..., rank_halfway:], spread_ranks[..., :rank_halfway]
    ).reshape(slots, 2 * tenant_list * rank_halfway)
    adapter_a_grad = product_leading(input_rows, mine_cols).reshape(
        1, quarter, 2, tenant_list, rank_halfway
    )
    returned = lax.all_to_all(slot_grad, "expert", split_axis=0, concat_axis=0, tiled=True)
    slot_rows = returned.reshape(experts * capacity, quarter)
    input_grad = product_leading(select_bf, slot_rows).astype(jnp.bfloat16)
    return (input_grad, adapter_a_grad, adapter_b_grad)


F32 = jnp.float32
BF16 = jnp.bfloat16
VMEM = pl.BlockSpec(memory_space=pltpu.VMEM)
HBM = pl.BlockSpec(memory_space=pltpu.HBM)
LONG = 20_000_000_000


def local_call(body, outs, operands, scratch=(), flops=0, moved=0, far=0, far_outs=0):
    operands = [
        pltpu.with_memory_space_constraint(array, pltpu.HBM) if k < far else array
        for k, array in enumerate(operands)
    ]
    return pl.pallas_call(
        body,
        out_shape=[jax.ShapeDtypeStruct(shape, kind) for shape, kind in outs],
        in_specs=[HBM] * far + [VMEM] * (len(operands) - far),
        out_specs=[HBM] * far_outs + [VMEM] * (len(outs) - far_outs),
        scratch_shapes=list(scratch),
        cost_estimate=pl.CostEstimate(flops=flops, bytes_accessed=moved, transcendentals=0),
        compiler_params=pltpu.CompilerParams(vmem_limit_bytes=16 << 20),
    )(*operands)


def dot_plain(left, right):
    return lax.dot_general(left, right, (((1,), (0,)), ((), ())), preferred_element_type=F32)


def swap(array, axis, offset):
    return lax.ppermute(array, axis, [(i, i ^ offset) for i in range(lax.axis_size(axis))])


def pack_body(
    x_ref, dy_ref, routes_ref, weight_ref, tenant_ref, out_ref, routes, weight, tenant, arrived
):
    width = x_ref.shape[1]
    topk, count = routes_ref.shape
    copies = [
        pltpu.make_async_copy(source, target, arrived.at[k])
        for k, (source, target) in enumerate(
            (
                (routes_ref, routes),
                (weight_ref, weight),
                (tenant_ref, tenant),
                (x_ref, out_ref.at[:, :width]),
                (dy_ref, out_ref.at[:, width : 2 * width]),
            )
        )
    ]
    for copy in copies:
        copy.start()
    for copy in copies[:3]:
        copy.wait()
    tags = [routes[...].astype(F32), weight[...].astype(F32), tenant[...].astype(F32)]
    rows = 2 * topk + 1
    tags = jnp.concatenate(tags + [jnp.zeros((count - rows, count), F32)], axis=0)
    tags = jnp.concatenate([tags, jnp.zeros((count, 128 - count), F32)], axis=1)
    out_ref[:, 2 * width :] = tags.astype(BF16)
    for copy in copies[3:]:
        copy.wait()


def stage_body(*refs):
    count = (len(refs) - 2) // 2
    sources, targets, maps, arrived = refs[:count], refs[count : 2 * count], refs[-2], refs[-1]
    copies = [
        pltpu.make_async_copy(source, target, arrived.at[k])
        for k, (source, target) in enumerate(zip(sources, targets[:-1] + (maps,)))
    ]
    for copy in copies:
        copy.start()
    copies[-1].wait()
    targets[-1][...] = dot_plain(rank_order(maps.shape[0], False), maps[...]).astype(BF16)
    for copy in copies[:-1]:
        copy.wait()


def rank_order(lanes, columns):
    at = lax.broadcasted_iota(jnp.int32, (lanes, lanes), 0 if columns else 1)
    place = lax.broadcasted_iota(jnp.int32, (lanes, lanes), 1 if columns else 0)
    if not columns:
        at, place = place, at
    source = lax.rem(place // 8, 2) * (lanes // 2) + (place // 16) * 8 + lax.rem(place, 8)
    return (at == source).astype(BF16)


def forward_body(*refs):
    gate_ref, up_ref, down_ref, mine_ref, other_ref, total_ref = refs[-6:]
    width, hidden = gate_ref.shape
    blocks = [ref[...].astype(F32) for ref in refs[:-6]]
    upper = lax.rem(lax.axis_index("expert"), 2)
    x = jnp.concatenate([block[:, :width] for block in blocks], axis=0).astype(BF16)
    dy = jnp.concatenate([block[:, width : 2 * width] for block in blocks], axis=0).astype(BF16)
    total_ref[:, :hidden] = dot_plain(x, gate_ref[...]).astype(BF16)
    total_ref[:, hidden : 2 * hidden] = dot_plain(x, up_ref[...]).astype(BF16)
    total_ref[:, 2 * hidden : 3 * hidden] = product_trailing(dy, down_ref[...]).astype(BF16)
    mine = product_trailing(x, mine_ref[...])
    other = product_trailing(x, other_ref[...])
    low = jnp.where(upper == 1, other, mine)
    high = jnp.where(upper == 1, mine, other)
    total_ref[:, 3 * hidden :] = jnp.concatenate([low, high], axis=1).astype(BF16)


def forward_rest_body(*refs):
    before_ref, total_ref, low_ref, high_ref = refs[-4:]
    half = low_ref.shape[0]
    forward_body(*refs[:-4], total_ref)
    low_ref[...] = before_ref[:half]
    high_ref[...] = before_ref[half:]


def pair_body(high_ref, high_taken_ref, low_ref, low_taken_ref, low_out_ref, high_out_ref):
    low = low_ref[...].astype(F32) + low_taken_ref[...].astype(F32)
    high = high_ref[...].astype(F32) + high_taken_ref[...].astype(F32)
    low_out_ref[...] = low.astype(BF16)
    high_out_ref[...] = high.astype(BF16)


def tags_body(topk, *refs):
    x_ref, tag_ref = refs[-2:]
    width = x_ref.shape[1]
    blocks = [ref[...].astype(F32) for ref in refs[:-2]]
    count = blocks[0].shape[0]
    slots = count * len(blocks)
    expert = (lax.axis_index("expert") // 2).astype(F32)
    x_ref[...] = jnp.concatenate([block[:, :width] for block in blocks], axis=0).astype(BF16)
    eye = (
        lax.broadcasted_iota(jnp.int32, (count, 128), 0)
        == lax.broadcasted_iota(jnp.int32, (count, 128), 1)
    ).astype(BF16)
    tags = jnp.concatenate(
        [product_leading(block[:, 2 * width :].astype(BF16), eye)[:count] for block in blocks],
        axis=0,
    )
    prob = jnp.zeros((slots, 1), F32)
    for k in range(topk):
        prob += jnp.where(tags[:, k : k + 1] == expert, tags[:, topk + k : topk + k + 1], 0.0)
    lane = lax.broadcasted_iota(jnp.int32, (slots, 128), 1)
    tenant = tags[:, 2 * topk : 2 * topk + 1]
    tag_ref[...] = jnp.where(lane == 0, prob, jnp.where(lane == 1, tenant, 0.0))


def lane_masks(tenant, shape, ranks):
    lane = lax.broadcasted_iota(jnp.int32, shape, 1)
    half = shape[1] // 2
    inner = lax.rem(lane, half)
    is_gate = inner < half // 2
    tenant_of = lax.rem(inner, half // 2) // ranks
    return is_gate, tenant_of.astype(F32) == tenant


def backward_rows(
    ranks,
    rows,
    total,
    tag_ref,
    gate_ref,
    up_ref,
    mine_ref,
    other_ref,
    maps_ref,
    rows_ref,
    back_ref,
):
    hidden = gate_ref.shape[1]
    half = mine_ref.shape[0]
    upper = lax.rem(lax.axis_index("expert"), 2)
    tags = tag_ref[rows, :]
    low = total[:, 3 * hidden :]
    is_gate, keep = lane_masks(tags[:, 1:2], low.shape, ranks)
    low = jnp.where(keep, low, 0.0).astype(BF16)
    low_wide = low.astype(F32)
    maps = maps_ref[...]
    gate = total[:, :hidden] + ADAPTER_SCALE * dot_plain(
        jnp.where(is_gate, low_wide, 0.0).astype(BF16), maps
    )
    up = total[:, hidden : 2 * hidden] + ADAPTER_SCALE * dot_plain(
        jnp.where(is_gate, 0.0, low_wide).astype(BF16), maps
    )
    act = tags[:, :1] * total[:, 2 * hidden : 3 * hidden]
    sig = jax.nn.sigmoid(gate)
    gate_grad = (act * up * sig * (1.0 + gate * (1.0 - sig))).astype(BF16)
    up_grad = (act * gate * sig).astype(BF16)
    rows_ref[:, :hidden] = gate_grad
    rows_ref[:, hidden : 2 * hidden] = up_grad
    rows_ref[:, 2 * hidden :] = low
    back_gate = product_trailing(gate_grad, maps)
    back_up = product_trailing(up_grad, maps)
    back = ADAPTER_SCALE * jnp.where(keep, jnp.where(is_gate, back_gate, back_up), 0.0)
    low, high = back[:, :half], back[:, half:]
    mine = jnp.where(upper == 1, high, low)
    other = jnp.where(upper == 1, low, high)
    back_ref[...] = jnp.concatenate([mine, other], axis=1)
    total = product_trailing(gate_grad, gate_ref[...])
    total += product_trailing(up_grad, up_ref[...])
    total += dot_plain(mine.astype(BF16), mine_ref[...])
    return total + dot_plain(other.astype(BF16), other_ref[...])


def backward_body(ranks, own_ref, first_ref, second_ref, third_ref, *refs):
    give_ref, rows_ref, back_ref = refs[-3:]
    count, lanes = back_ref.shape
    width = give_ref.shape[1] - lanes // 2
    total = (own_ref[...].astype(F32) + first_ref[...].astype(F32)) + (
        second_ref[...].astype(F32) + third_ref[...].astype(F32)
    )
    total = backward_rows(ranks, slice(0, count), total, *refs[:-3], rows_ref, back_ref)
    give_ref[:, :width] = total.astype(BF16)
    give_ref[:, width:] = back_ref[:, lanes // 2 :].astype(BF16)


def backward_rest_body(ranks, low_ref, low_taken_ref, high_ref, high_taken_ref, *refs):
    keep_ref, back_give_ref, rows_ref, back_ref = refs[-4:]
    count, lanes = back_ref.shape
    low = low_ref[...].astype(F32) + low_taken_ref[...].astype(F32)
    high = high_ref[...].astype(F32) + high_taken_ref[...].astype(F32)
    total = jnp.concatenate([low, high], axis=0)
    keep_ref[...] = backward_rows(
        ranks, slice(count, 2 * count), total, *refs[:-4], rows_ref, back_ref
    )
    back_give_ref[...] = back_ref[:, lanes // 2 :]


def join_body(keep_ref, taken_ref, own_ref, first_ref, second_ref, third_ref):
    count = own_ref.shape[0]
    total = keep_ref[...] + taken_ref[:, : own_ref.shape[1]].astype(F32)
    for k, ref in enumerate((own_ref, first_ref, second_ref, third_ref)):
        ref[...] = total[k * count : (k + 1) * count].astype(ref.dtype)


def finish_body(own_ref, third_ref, second_ref, first_ref, out_ref):
    total = (own_ref[...] + first_ref[...].astype(F32)) + (
        second_ref[...].astype(F32) + third_ref[...].astype(F32)
    )
    out_ref[...] = total.astype(BF16)


def maps_grad_body(
    rows_ref,
    rest_rows_ref,
    back_ref,
    rest_back_ref,
    taken_ref,
    rest_taken_ref,
    x_ref,
    maps_out_ref,
    inputs_out_ref,
    maps,
    inputs,
    arrived,
):
    lanes, hidden = maps.shape
    half = lanes // 2
    width = x_ref.shape[1]
    copies = [
        pltpu.make_async_copy(maps, maps_out_ref, arrived.at[0]),
        pltpu.make_async_copy(inputs, inputs_out_ref, arrived.at[1]),
    ]
    taken = jnp.concatenate([rest_taken_ref[...], taken_ref[:, width:].astype(F32)], axis=0)
    back = jnp.concatenate([back_ref[:, :half], rest_back_ref[:, :half]], axis=0)
    inputs[...] = product_leading((back + taken).astype(BF16), x_ref[...])
    copies[1].start()
    rows = jnp.concatenate([rows_ref[...], rest_rows_ref[...]], axis=0)
    low = dot_plain(rows[:, 2 * hidden :], rank_order(lanes, True)).astype(BF16)
    maps[:half] = ADAPTER_SCALE * product_leading(low[:, :half], rows[:, :hidden])
    maps[half:] = ADAPTER_SCALE * product_leading(low[:, half:], rows[:, hidden : 2 * hidden])
    copies[0].start()
    for copy in copies:
        copy.wait()


def dense_shards(
    tokens,
    output_gradient,
    routes,
    router_expert_weight,
    tenant,
    gate_weight,
    up_weight,
    down_weight,
    adapter_input_maps,
    adapter_output_maps,
):
    devices = lax.axis_size("expert")
    chips = devices // 2
    count, width = tokens.shape
    topk = routes.shape[1]
    tenants, rank, hidden = adapter_output_maps.shape[2:]
    ranks = rank // 2
    lanes = 2 * tenants * rank
    slots = devices * count
    mine_cols = adapter_input_maps[0].transpose(1, 2, 3, 0).reshape(lanes // 2, width)
    other_cols = swap(mine_cols, "expert", 1)
    (packed,) = local_call(
        pack_body,
        [((count, 2 * width + 128), BF16)],
        (tokens, output_gradient, routes.T, router_expert_weight.T, tenant[None, :]),
        scratch=[
            pltpu.VMEM((topk, count), jnp.int32),
            pltpu.VMEM((topk, count), BF16),
            pltpu.VMEM((1, count), jnp.int32),
            pltpu.SemaphoreType.DMA((5,)),
        ],
        far=5,
    )
    stored = (
        gate_weight[0],
        up_weight[0],
        down_weight[0],
        mine_cols,
        adapter_output_maps.reshape(lanes, hidden),
    )
    gate, up, down, mine_cols, maps = local_call(
        stage_body,
        [(array.shape, BF16) for array in stored],
        stored,
        scratch=[pltpu.VMEM((lanes, hidden), BF16), pltpu.SemaphoreType.DMA((len(stored),))],
        moved=sum(2 * array.size for array in stored),
        far=len(stored),
    )
    same_core = [packed] + [swap(packed, "expert", 2 * k) for k in range(1, chips)]
    same_core[-1], (gate, up, down, mine_cols, maps) = lax.optimization_barrier(
        (same_core[-1], (gate, up, down, mine_cols, maps))
    )
    other_core = [swap(block, "expert", 1) for block in same_core]
    columns = 3 * hidden + lanes
    weights = (gate, up, down, mine_cols, other_cols)
    (before,) = local_call(
        forward_body,
        [((slots // 2, columns), BF16)],
        (*same_core, *weights),
        flops=slots * width * columns,
    )
    part = slots // 4
    own, low, high = local_call(
        forward_rest_body,
        [((slots // 2, columns), BF16), ((part, columns), BF16), ((part, columns), BF16)],
        (*other_core, *weights, before),
        flops=slots * width * columns,
    )
    low_taken, high_taken = swap(low, "dp", 1), swap(high, "dp", 2)
    sums = [own] + [swap(own, "dp", k) for k in (1, 2, 3)]
    low, high = local_call(
        pair_body,
        [((part, columns), BF16)] * 2,
        (high, high_taken, low, low_taken),
        flops=LONG,
    )
    rest_sums = [low, swap(low, "dp", 2), high, swap(high, "dp", 1)]
    x, tags = local_call(
        functools.partial(tags_body, topk),
        [((slots, width), BF16), ((slots, 128), F32)],
        (*other_core, *same_core),
    )
    shared = (tags, gate, up, mine_cols, other_cols, maps)
    outs = [((slots // 2, 2 * hidden + lanes), BF16), ((slots // 2, lanes), F32)]
    give, rows, back = local_call(
        functools.partial(backward_body, ranks),
        [((slots // 2, width + lanes // 2), BF16)] + outs,
        (*sums, *shared),
        flops=LONG,
    )
    taken = swap(give, "expert", 1)
    keep, back_give, rest_rows, rest_back = local_call(
        functools.partial(backward_rest_body, ranks),
        [((slots // 2, width), F32), ((slots // 2, lanes // 2), F32)] + outs,
        (*rest_sums, *shared),
        flops=LONG,
    )
    back_taken = swap(back_give, "expert", 1)
    own, first, second, third = local_call(
        join_body,
        [((count, width), F32)] + [((count, width), BF16)] * 3,
        (keep, taken),
    )
    third, second = swap(third, "expert", 6), swap(second, "expert", 4)
    returned = [own, third, second, swap(first, "expert", 2)]
    maps_grad, input_maps_grad = local_call(
        maps_grad_body,
        [((lanes, hidden), F32), ((lanes // 2, width), F32)],
        (rows, rest_rows, back, rest_back, taken, back_taken, x),
        scratch=[
            pltpu.VMEM((lanes, hidden), F32),
            pltpu.VMEM((lanes // 2, width), F32),
            pltpu.SemaphoreType.DMA((2,)),
        ],
        far_outs=2,
        flops=LONG,
    )
    (input_grad,) = local_call(finish_body, [((count, width), BF16)], returned)
    adapter_a_grad = (
        input_maps_grad.reshape(2, tenants, ranks, width).transpose(3, 0, 1, 2)[None]
    )
    adapter_b_grad = maps_grad.reshape(1, 2, tenants, rank, hidden)
    return input_grad, adapter_a_grad, adapter_b_grad


def shards(*arrays):
    tokens, routes, maps = arrays[0], arrays[2], arrays[9]
    devices = lax.axis_size("expert")
    capacity = 4 * tokens.shape[0] * routes.shape[1] // devices
    if (
        capacity >= tokens.shape[0]
        and devices == 8
        and lax.axis_size("dp") == 4
        and tokens.shape[0] == 8
        and maps.shape[2] * maps.shape[3] == 64
    ):
        return dense_shards(*arrays)
    return routed_shards(*arrays)


def solution(mesh):
    placed = (
        P("expert", "dp"),
        P("expert", "dp"),
        P("expert", None),
        P("expert", None),
        P("expert"),
        P("expert", "dp", None),
        P("expert", "dp", None),
        P("expert", None, "dp"),
        P("expert", "dp", None, None, None),
        P("expert", None, None, None, None),
    )
    return jax.shard_map(
        shards,
        mesh=mesh,
        in_specs=placed,
        out_specs=(
            P("expert", "dp"),
            P("expert", "dp", None, None, None),
            P("expert", None, None, None, None),
        ),
        check_vma=False,
    )
```

```python
import functools

import jax
import jax.numpy as jnp
from jax import lax
from jax.experimental import pallas as pl
from jax.experimental.pallas import tpu as pltpu
from jax.sharding import PartitionSpec as P

ADAPTER_SCALE = 2.0


def partner(shard, axis, bit):
    return lax.ppermute(shard, axis, [(i, i ^ 1 << bit) for i in range(lax.axis_size(axis))])


def product_leading(left, right):
    return lax.dot_general(
        left, right, (((0,), (0,)), ((), ())), preferred_element_type=jnp.float32
    )


def product_trailing(left, right):
    return lax.dot_general(
        left, right, (((1,), (1,)), ((), ())), preferred_element_type=jnp.float32
    )


def order_halves(mine, other, upper):
    return (jnp.where(upper, other, mine), jnp.where(upper, mine, other))


def spread(values, tenant_mask, tenant_list, adapter_rank_width):
    count = values.shape[0]
    wide = tenant_mask[:, None, :, None] * values.astype(jnp.float32).reshape(
        count, 2, 1, adapter_rank_width
    )
    return wide.reshape(count, 2, tenant_list * adapter_rank_width).astype(jnp.bfloat16)


def routed_shards(
    tokens,
    output_gradient,
    routes,
    router_expert_weight,
    tenant,
    gate_weight,
    up_weight,
    down_weight,
    adapter_input_maps,
    adapter_output_maps,
):
    devices = lax.axis_size("expert")
    experts = devices // 2
    tok_col, quarter = tokens.shape
    topk = routes.shape[1]
    tenant_list = adapter_output_maps.shape[2]
    adapter_rank_width = adapter_output_maps.shape[3]
    hidden_halfway = adapter_output_maps.shape[4]
    rank_halfway = adapter_rank_width // 2
    capacity = 2 * tok_col * topk // experts
    half_cap = capacity // 2
    slots = devices * capacity
    upper = lax.axis_index("expert") % 2 == 1
    flat_route = routes.reshape(-1)
    expert_hot = (flat_route[:, None] == jnp.arange(experts, dtype=jnp.int32)[None, :]).astype(
        jnp.int32
    )
    earlier = jnp.cumsum(expert_hot, axis=0) - expert_hot
    position = jnp.sum(earlier * expert_hot, axis=1)
    slot_of = (flat_route * capacity + position).reshape(tok_col, topk)
    slot_range = jnp.arange(experts * capacity, dtype=jnp.int32)
    hits = (slot_range[:, None, None] == slot_of[None, :, :]).astype(jnp.float32)
    select_tok = jnp.sum(hits, axis=2)
    prob_tok = jnp.sum(hits * router_expert_weight.astype(jnp.float32)[None, :, :], axis=2)
    tenant_hot = (tenant[:, None] == jnp.arange(tenant_list, dtype=jnp.int32)[None, :]).astype(
        jnp.float32
    )
    select_bf = select_tok.astype(jnp.bfloat16)
    send_rows = jnp.dot(select_bf, tokens, preferred_element_type=jnp.float32).astype(jnp.bfloat16)
    send_grad = jnp.dot(select_bf, output_gradient, preferred_element_type=jnp.float32).astype(
        jnp.bfloat16
    )
    send_tag = jnp.dot(prob_tok, tenant_hot, precision=lax.Precision.HIGHEST).astype(jnp.bfloat16)

    def doubled(block):
        wide = block.reshape(experts, 1, capacity, block.shape[1])
        return jnp.broadcast_to(wide, (experts, 2, capacity, block.shape[1])).reshape(
            devices, capacity, block.shape[1]
        )

    got_rows, got_grad, got_tag = (
        lax.all_to_all(doubled(send_rows), "expert", split_axis=0, concat_axis=0, tiled=True),
        lax.all_to_all(doubled(send_grad), "expert", split_axis=0, concat_axis=0, tiled=True),
        lax.all_to_all(doubled(send_tag), "expert", split_axis=0, concat_axis=0, tiled=True),
    )
    input_rows = got_rows.reshape(slots, quarter)
    rows_dy = got_grad.reshape(slots, quarter)
    tags = got_tag.reshape(slots, tenant_list).astype(jnp.float32)
    tenant_mask = (tags > 0).astype(jnp.float32)
    slot_prob = jnp.sum(tags, axis=1)
    adapter_local = adapter_input_maps[0]
    adapter_other = partner(adapter_local, "expert", 0)
    low_rank, high_rank = order_halves(adapter_local, adapter_other, upper)
    adapter_cols = jnp.concatenate([low_rank, high_rank], axis=-1).reshape(
        quarter, 2 * tenant_list * adapter_rank_width
    )
    gate_output_map = adapter_output_maps[0, 0].reshape(
        tenant_list * adapter_rank_width, hidden_halfway
    )
    up_output_map = adapter_output_maps[0, 1].reshape(
        tenant_list * adapter_rank_width, hidden_halfway
    )
    gate_part = jnp.dot(input_rows, gate_weight[0], preferred_element_type=jnp.float32)
    up_part = jnp.dot(input_rows, up_weight[0], preferred_element_type=jnp.float32)
    act_part = product_trailing(rows_dy, down_weight[0])
    proj_all = jnp.dot(input_rows, adapter_cols, preferred_element_type=jnp.float32).reshape(
        slots, 2, tenant_list, adapter_rank_width
    )
    proj_part = jnp.sum(proj_all * tenant_mask[:, None, :, None], axis=2).reshape(
        slots, 2 * adapter_rank_width
    )
    gate_total, up_total, act_sum, proj_sum = lax.psum(
        (gate_part, up_part, act_part, proj_part), "dp"
    )
    proj_low = proj_sum.astype(jnp.bfloat16)
    spread_in = spread(proj_low, tenant_mask, tenant_list, adapter_rank_width)
    gate_preactivation = gate_total + ADAPTER_SCALE * jnp.dot(
        spread_in[:, 0], gate_output_map, preferred_element_type=jnp.float32
    )
    up_preactivation = up_total + ADAPTER_SCALE * jnp.dot(
        spread_in[:, 1], up_output_map, preferred_element_type=jnp.float32
    )
    act_grad = slot_prob[:, None] * act_sum
    gate_sig = jax.nn.sigmoid(gate_preactivation)
    gate_gradient = (
        act_grad * up_preactivation * gate_sig * (1.0 + gate_preactivation * (1.0 - gate_sig))
    ).astype(jnp.bfloat16)
    up_gradient = (act_grad * gate_preactivation * gate_sig).astype(jnp.bfloat16)
    gate_gradient, up_gradient, proj_low = (gate_gradient, up_gradient, proj_low)
    projection_spread = spread(proj_low, tenant_mask, tenant_list, adapter_rank_width)
    gate_output_map_gradient = ADAPTER_SCALE * product_leading(
        projection_spread[:, 0], gate_gradient
    )
    up_output_map_gradient = ADAPTER_SCALE * product_leading(projection_spread[:, 1], up_gradient)
    adapter_b_grad = jnp.stack([gate_output_map_gradient, up_output_map_gradient]).reshape(
        1, 2, tenant_list, adapter_rank_width, hidden_halfway
    )
    backward_total = ADAPTER_SCALE * jnp.stack(
        [
            product_trailing(gate_gradient, gate_output_map),
            product_trailing(up_gradient, up_output_map),
        ],
        axis=1,
    )
    back_part = jnp.sum(
        backward_total.reshape(slots, 2, tenant_list, adapter_rank_width)
        * tenant_mask[:, None, :, None],
        axis=2,
    ).reshape(slots, 2 * adapter_rank_width)
    input_part = product_trailing(gate_gradient, gate_weight[0]) + product_trailing(
        up_gradient, up_weight[0]
    )
    by_source = input_part.reshape(devices, capacity, quarter)
    first_half = by_source[:, :half_cap]
    second_half = by_source[:, half_cap:]
    keep_half = jnp.where(upper, second_half, first_half)
    give_half = jnp.where(upper, first_half, second_half)
    taken_half, back_other = partner((give_half, back_part), "expert", 0)
    input_half = keep_half + taken_half
    back_low = (back_part + back_other).astype(jnp.bfloat16)
    back_spread = spread(back_low, tenant_mask, tenant_list, adapter_rank_width)
    spread_rows = back_spread.reshape(devices, capacity, 2 * tenant_list * adapter_rank_width)
    spread_half = jnp.where(upper, spread_rows[:, half_cap:], spread_rows[:, :half_cap]).reshape(
        devices * half_cap, 2 * tenant_list * adapter_rank_width
    )
    adapter_term = product_trailing(spread_half, adapter_cols).reshape(devices, half_cap, quarter)
    slot_grad = (input_half + adapter_term).astype(jnp.bfloat16)
    spread_ranks = back_spread.reshape(slots, 2, tenant_list, adapter_rank_width)
    mine_cols = jnp.where(
        upper, spread_ranks[..., rank_halfway:], spread_ranks[..., :rank_halfway]
    ).reshape(slots, 2 * tenant_list * rank_halfway)
    adapter_a_grad = product_leading(input_rows, mine_cols).reshape(
        1, quarter, 2, tenant_list, rank_halfway
    )
    returned = lax.all_to_all(slot_grad, "expert", split_axis=0, concat_axis=0, tiled=True)
    slot_rows = returned.reshape(experts * capacity, quarter)
    input_grad = product_leading(select_bf, slot_rows).astype(jnp.bfloat16)
    return (input_grad, adapter_a_grad, adapter_b_grad)


F32 = jnp.float32
BF16 = jnp.bfloat16
VMEM = pl.BlockSpec(memory_space=pltpu.VMEM)
HBM = pl.BlockSpec(memory_space=pltpu.HBM)
LONG = 20_000_000_000


def local_call(body, outs, operands, scratch=(), flops=0, moved=0, far=0, far_outs=0):
    operands = [
        pltpu.with_memory_space_constraint(array, pltpu.HBM) if k < far else array
        for k, array in enumerate(operands)
    ]
    return pl.pallas_call(
        body,
        out_shape=[jax.ShapeDtypeStruct(shape, kind) for shape, kind in outs],
        in_specs=[HBM] * far + [VMEM] * (len(operands) - far),
        out_specs=[HBM] * far_outs + [VMEM] * (len(outs) - far_outs),
        scratch_shapes=list(scratch),
        cost_estimate=pl.CostEstimate(flops=flops, bytes_accessed=moved, transcendentals=0),
        compiler_params=pltpu.CompilerParams(vmem_limit_bytes=16 << 20),
    )(*operands)


def dot_plain(left, right):
    return lax.dot_general(left, right, (((1,), (0,)), ((), ())), preferred_element_type=F32)


def swap(array, axis, offset):
    return lax.ppermute(array, axis, [(i, i ^ offset) for i in range(lax.axis_size(axis))])


def pack_body(
    x_ref, dy_ref, routes_ref, weight_ref, tenant_ref, out_ref, routes, weight, tenant, arrived
):
    width = x_ref.shape[1]
    topk, count = routes_ref.shape
    copies = [
        pltpu.make_async_copy(source, target, arrived.at[k])
        for k, (source, target) in enumerate(
            (
                (routes_ref, routes),
                (weight_ref, weight),
                (tenant_ref, tenant),
                (x_ref, out_ref.at[:, :width]),
                (dy_ref, out_ref.at[:, width : 2 * width]),
            )
        )
    ]
    for copy in copies:
        copy.start()
    for copy in copies[:3]:
        copy.wait()
    tags = [routes[...].astype(F32), weight[...].astype(F32), tenant[...].astype(F32)]
    rows = 2 * topk + 1
    tags = jnp.concatenate(tags + [jnp.zeros((count - rows, count), F32)], axis=0)
    tags = jnp.concatenate([tags, jnp.zeros((count, 128 - count), F32)], axis=1)
    out_ref[:, 2 * width :] = tags.astype(BF16)
    for copy in copies[3:]:
        copy.wait()


def stage_body(*refs):
    count = (len(refs) - 2) // 2
    sources, targets, maps, arrived = refs[:count], refs[count : 2 * count], refs[-2], refs[-1]
    copies = [
        pltpu.make_async_copy(source, target, arrived.at[k])
        for k, (source, target) in enumerate(zip(sources, targets[:-1] + (maps,)))
    ]
    for copy in copies:
        copy.start()
    copies[-1].wait()
    targets[-1][...] = dot_plain(rank_order(maps.shape[0], False), maps[...]).astype(BF16)
    for copy in copies[:-1]:
        copy.wait()


def rank_order(lanes, columns):
    at = lax.broadcasted_iota(jnp.int32, (lanes, lanes), 0 if columns else 1)
    place = lax.broadcasted_iota(jnp.int32, (lanes, lanes), 1 if columns else 0)
    if not columns:
        at, place = place, at
    source = lax.rem(place // 8, 2) * (lanes // 2) + (place // 16) * 8 + lax.rem(place, 8)
    return (at == source).astype(BF16)


def forward_body(*refs):
    gate_ref, up_ref, down_ref, mine_ref, other_ref, total_ref = refs[-6:]
    width, hidden = gate_ref.shape
    blocks = [ref[...].astype(F32) for ref in refs[:-6]]
    upper = lax.rem(lax.axis_index("expert"), 2)
    x = jnp.concatenate([block[:, :width] for block in blocks], axis=0).astype(BF16)
    dy = jnp.concatenate([block[:, width : 2 * width] for block in blocks], axis=0).astype(BF16)
    total_ref[:, :hidden] = dot_plain(x, gate_ref[...]).astype(BF16)
    total_ref[:, hidden : 2 * hidden] = dot_plain(x, up_ref[...]).astype(BF16)
    total_ref[:, 2 * hidden : 3 * hidden] = product_trailing(dy, down_ref[...]).astype(BF16)
    mine = product_trailing(x, mine_ref[...])
    other = product_trailing(x, other_ref[...])
    low = jnp.where(upper == 1, other, mine)
    high = jnp.where(upper == 1, mine, other)
    total_ref[:, 3 * hidden :] = jnp.concatenate([low, high], axis=1).astype(BF16)


def forward_rest_body(*refs):
    before_ref, total_ref, mine_total_ref = refs[-3:]
    forward_body(*refs[:-3], total_ref)
    mine_total_ref[...] = before_ref[...]


def pair_body(own_ref, taken_ref, out_ref):
    out_ref[...] = (own_ref[...].astype(F32) + taken_ref[...].astype(F32)).astype(BF16)


def tags_body(topk, *refs):
    x_ref, tag_ref = refs[-2:]
    width = x_ref.shape[1]
    blocks = [ref[...].astype(F32) for ref in refs[:-2]]
    count = blocks[0].shape[0]
    slots = count * len(blocks)
    expert = (lax.axis_index("expert") // 2).astype(F32)
    x_ref[...] = jnp.concatenate([block[:, :width] for block in blocks], axis=0).astype(BF16)
    eye = (
        lax.broadcasted_iota(jnp.int32, (count, 128), 0)
        == lax.broadcasted_iota(jnp.int32, (count, 128), 1)
    ).astype(BF16)
    tags = jnp.concatenate(
        [product_leading(block[:, 2 * width :].astype(BF16), eye)[:count] for block in blocks],
        axis=0,
    )
    prob = jnp.zeros((slots, 1), F32)
    for k in range(topk):
        prob += jnp.where(tags[:, k : k + 1] == expert, tags[:, topk + k : topk + k + 1], 0.0)
    lane = lax.broadcasted_iota(jnp.int32, (slots, 128), 1)
    tenant = tags[:, 2 * topk : 2 * topk + 1]
    tag_ref[...] = jnp.where(lane == 0, prob, jnp.where(lane == 1, tenant, 0.0))


def lane_masks(tenant, shape, ranks):
    lane = lax.broadcasted_iota(jnp.int32, shape, 1)
    half = shape[1] // 2
    inner = lax.rem(lane, half)
    is_gate = inner < half // 2
    tenant_of = lax.rem(inner, half // 2) // ranks
    return is_gate, tenant_of.astype(F32) == tenant


def backward_rows(
    ranks,
    rows,
    total,
    tag_ref,
    gate_ref,
    up_ref,
    mine_ref,
    other_ref,
    maps_ref,
    rows_ref,
    back_ref,
):
    hidden = gate_ref.shape[1]
    half = mine_ref.shape[0]
    upper = lax.rem(lax.axis_index("expert"), 2)
    tags = tag_ref[rows, :]
    low = total[:, 3 * hidden :]
    is_gate, keep = lane_masks(tags[:, 1:2], low.shape, ranks)
    low = jnp.where(keep, low, 0.0).astype(BF16)
    low_wide = low.astype(F32)
    maps = maps_ref[...]
    gate = total[:, :hidden] + ADAPTER_SCALE * dot_plain(
        jnp.where(is_gate, low_wide, 0.0).astype(BF16), maps
    )
    up = total[:, hidden : 2 * hidden] + ADAPTER_SCALE * dot_plain(
        jnp.where(is_gate, 0.0, low_wide).astype(BF16), maps
    )
    act = tags[:, :1] * total[:, 2 * hidden : 3 * hidden]
    sig = jax.nn.sigmoid(gate)
    gate_grad = (act * up * sig * (1.0 + gate * (1.0 - sig))).astype(BF16)
    up_grad = (act * gate * sig).astype(BF16)
    rows_ref[:, :hidden] = gate_grad
    rows_ref[:, hidden : 2 * hidden] = up_grad
    rows_ref[:, 2 * hidden :] = low
    back_gate = product_trailing(gate_grad, maps)
    back_up = product_trailing(up_grad, maps)
    back = ADAPTER_SCALE * jnp.where(keep, jnp.where(is_gate, back_gate, back_up), 0.0)
    low, high = back[:, :half], back[:, half:]
    mine = jnp.where(upper == 1, high, low)
    other = jnp.where(upper == 1, low, high)
    back_ref[...] = jnp.concatenate([mine, other], axis=1)
    total = product_trailing(gate_grad, gate_ref[...])
    total += product_trailing(up_grad, up_ref[...])
    total += dot_plain(mine.astype(BF16), mine_ref[...])
    return total + dot_plain(other.astype(BF16), other_ref[...])


def backward_body(ranks, own_ref, second_ref, first_ref, third_ref, *refs):
    give_ref, rows_ref, back_ref = refs[-3:]
    count, lanes = back_ref.shape
    width = give_ref.shape[1] - lanes // 2
    total = (own_ref[...].astype(F32) + first_ref[...].astype(F32)) + (
        second_ref[...].astype(F32) + third_ref[...].astype(F32)
    )
    total = backward_rows(ranks, slice(0, count), total, *refs[:-3], rows_ref, back_ref)
    give_ref[:, :width] = total.astype(BF16)
    give_ref[:, width:] = back_ref[:, lanes // 2 :].astype(BF16)


def backward_rest_body(ranks, own_ref, pair_ref, *refs):
    keep_ref, back_give_ref, rows_ref, back_ref = refs[-4:]
    count, lanes = back_ref.shape
    total = own_ref[...].astype(F32) + pair_ref[...].astype(F32)
    keep_ref[...] = backward_rows(
        ranks, slice(count, 2 * count), total, *refs[:-4], rows_ref, back_ref
    )
    back_give_ref[...] = back_ref[:, lanes // 2 :]


def join_body(keep_ref, taken_ref, own_ref, first_ref, second_ref, third_ref):
    count = own_ref.shape[0]
    total = keep_ref[...] + taken_ref[:, : own_ref.shape[1]].astype(F32)
    for k, ref in enumerate((own_ref, first_ref, second_ref, third_ref)):
        ref[...] = total[k * count : (k + 1) * count].astype(ref.dtype)


def finish_body(own_ref, third_ref, second_ref, first_ref, out_ref):
    total = (own_ref[...] + first_ref[...].astype(F32)) + (
        second_ref[...].astype(F32) + third_ref[...].astype(F32)
    )
    out_ref[...] = total.astype(BF16)


def maps_grad_body(
    rows_ref,
    rest_rows_ref,
    back_ref,
    rest_back_ref,
    taken_ref,
    rest_taken_ref,
    x_ref,
    maps_out_ref,
    inputs_out_ref,
    maps,
    inputs,
    arrived,
):
    lanes, hidden = maps.shape
    half = lanes // 2
    width = x_ref.shape[1]
    copies = [
        pltpu.make_async_copy(maps, maps_out_ref, arrived.at[0]),
        pltpu.make_async_copy(inputs, inputs_out_ref, arrived.at[1]),
    ]
    taken = jnp.concatenate([rest_taken_ref[...], taken_ref[:, width:].astype(F32)], axis=0)
    back = jnp.concatenate([back_ref[:, :half], rest_back_ref[:, :half]], axis=0)
    inputs[...] = product_leading((back + taken).astype(BF16), x_ref[...])
    copies[1].start()
    rows = jnp.concatenate([rows_ref[...], rest_rows_ref[...]], axis=0)
    low = dot_plain(rows[:, 2 * hidden :], rank_order(lanes, True)).astype(BF16)
    maps[:half] = ADAPTER_SCALE * product_leading(low[:, :half], rows[:, :hidden])
    maps[half:] = ADAPTER_SCALE * product_leading(low[:, half:], rows[:, hidden : 2 * hidden])
    copies[0].start()
    for copy in copies:
        copy.wait()


def dense_shards(
    tokens,
    output_gradient,
    routes,
    router_expert_weight,
    tenant,
    gate_weight,
    up_weight,
    down_weight,
    adapter_input_maps,
    adapter_output_maps,
):
    devices = lax.axis_size("expert")
    chips = devices // 2
    count, width = tokens.shape
    topk = routes.shape[1]
    tenants, rank, hidden = adapter_output_maps.shape[2:]
    ranks = rank // 2
    lanes = 2 * tenants * rank
    slots = devices * count
    mine_cols = adapter_input_maps[0].transpose(1, 2, 3, 0).reshape(lanes // 2, width)
    other_cols = swap(mine_cols, "expert", 1)
    (packed,) = local_call(
        pack_body,
        [((count, 2 * width + 128), BF16)],
        (tokens, output_gradient, routes.T, router_expert_weight.T, tenant[None, :]),
        scratch=[
            pltpu.VMEM((topk, count), jnp.int32),
            pltpu.VMEM((topk, count), BF16),
            pltpu.VMEM((1, count), jnp.int32),
            pltpu.SemaphoreType.DMA((5,)),
        ],
        far=5,
    )
    stored = (
        gate_weight[0],
        up_weight[0],
        down_weight[0],
        mine_cols,
        adapter_output_maps.reshape(lanes, hidden),
    )
    gate, up, down, mine_cols, maps = local_call(
        stage_body,
        [(array.shape, BF16) for array in stored],
        stored,
        scratch=[pltpu.VMEM((lanes, hidden), BF16), pltpu.SemaphoreType.DMA((len(stored),))],
        moved=sum(2 * array.size for array in stored),
        far=len(stored),
    )
    same_core = [packed] + [swap(packed, "expert", 2 * k) for k in range(1, chips)]
    same_core[-1], (gate, up, down, mine_cols, maps) = lax.optimization_barrier(
        (same_core[-1], (gate, up, down, mine_cols, maps))
    )
    other_core = [swap(block, "expert", 1) for block in same_core]
    columns = 3 * hidden + lanes
    weights = (gate, up, down, mine_cols, other_cols)
    (before,) = local_call(
        forward_body,
        [((slots // 2, columns), BF16)],
        (*same_core, *weights),
        flops=slots * width * columns,
    )
    own, mine = local_call(
        forward_rest_body,
        [((slots // 2, columns), BF16)] * 2,
        (*other_core, *weights, before),
        flops=slots * width * columns,
    )
    sums = [own] + [swap(own, "dp", k) for k in (2, 1, 3)]
    (pair,) = local_call(
        pair_body,
        [((slots // 2, columns), BF16)],
        (mine, swap(mine, "dp", 2)),
        flops=LONG,
    )
    rest_sums = [pair, swap(pair, "dp", 1)]
    x, tags = local_call(
        functools.partial(tags_body, topk),
        [((slots, width), BF16), ((slots, 128), F32)],
        (*other_core, *same_core),
    )
    shared = (tags, gate, up, mine_cols, other_cols, maps)
    outs = [((slots // 2, 2 * hidden + lanes), BF16), ((slots // 2, lanes), F32)]
    give, rows, back = local_call(
        functools.partial(backward_body, ranks),
        [((slots // 2, width + lanes // 2), BF16)] + outs,
        (*sums, *shared),
        flops=LONG,
    )
    taken = swap(give, "expert", 1)
    keep, back_give, rest_rows, rest_back = local_call(
        functools.partial(backward_rest_body, ranks),
        [((slots // 2, width), F32), ((slots // 2, lanes // 2), F32)] + outs,
        (*rest_sums, *shared),
        flops=LONG,
    )
    back_taken = swap(back_give, "expert", 1)
    own, first, second, third = local_call(
        join_body,
        [((count, width), F32)] + [((count, width), BF16)] * 3,
        (keep, taken),
    )
    third, second = swap(third, "expert", 6), swap(second, "expert", 4)
    returned = [own, third, second, swap(first, "expert", 2)]
    maps_grad, input_maps_grad = local_call(
        maps_grad_body,
        [((lanes, hidden), F32), ((lanes // 2, width), F32)],
        (rows, rest_rows, back, rest_back, taken, back_taken, x),
        scratch=[
            pltpu.VMEM((lanes, hidden), F32),
            pltpu.VMEM((lanes // 2, width), F32),
            pltpu.SemaphoreType.DMA((2,)),
        ],
        far_outs=2,
        flops=LONG,
    )
    (input_grad,) = local_call(finish_body, [((count, width), BF16)], returned)
    adapter_a_grad = (
        input_maps_grad.reshape(2, tenants, ranks, width).transpose(3, 0, 1, 2)[None]
    )
    adapter_b_grad = maps_grad.reshape(1, 2, tenants, rank, hidden)
    return input_grad, adapter_a_grad, adapter_b_grad


def shards(*arrays):
    tokens, routes, maps = arrays[0], arrays[2], arrays[9]
    devices = lax.axis_size("expert")
    capacity = 4 * tokens.shape[0] * routes.shape[1] // devices
    if (
        capacity >= tokens.shape[0]
        and devices == 8
        and lax.axis_size("dp") == 4
        and tokens.shape[0] == 8
        and maps.shape[2] * maps.shape[3] == 64
    ):
        return dense_shards(*arrays)
    return routed_shards(*arrays)


def solution(mesh):
    placed = (
        P("expert", "dp"),
        P("expert", "dp"),
        P("expert", None),
        P("expert", None),
        P("expert"),
        P("expert", "dp", None),
        P("expert", "dp", None),
        P("expert", None, "dp"),
        P("expert", "dp", None, None, None),
        P("expert", None, None, None, None),
    )
    return jax.shard_map(
        shards,
        mesh=mesh,
        in_specs=placed,
        out_specs=(
            P("expert", "dp"),
            P("expert", "dp", None, None, None),
            P("expert", None, None, None, None),
        ),
        check_vma=False,
    )
```

```python
import functools

import jax
import jax.numpy as jnp
from jax import lax
from jax.experimental import pallas as pl
from jax.experimental.pallas import tpu as pltpu
from jax.sharding import PartitionSpec as P

ADAPTER_SCALE = 2.0


def partner(shard, axis, bit):
    return lax.ppermute(shard, axis, [(i, i ^ 1 << bit) for i in range(lax.axis_size(axis))])


def product_leading(left, right):
    return lax.dot_general(
        left, right, (((0,), (0,)), ((), ())), preferred_element_type=jnp.float32
    )


def product_trailing(left, right):
    return lax.dot_general(
        left, right, (((1,), (1,)), ((), ())), preferred_element_type=jnp.float32
    )


def order_halves(mine, other, upper):
    return (jnp.where(upper, other, mine), jnp.where(upper, mine, other))


def spread(values, tenant_mask, tenant_list, adapter_rank_width):
    count = values.shape[0]
    wide = tenant_mask[:, None, :, None] * values.astype(jnp.float32).reshape(
        count, 2, 1, adapter_rank_width
    )
    return wide.reshape(count, 2, tenant_list * adapter_rank_width).astype(jnp.bfloat16)


def routed_shards(
    tokens,
    output_gradient,
    routes,
    router_expert_weight,
    tenant,
    gate_weight,
    up_weight,
    down_weight,
    adapter_input_maps,
    adapter_output_maps,
):
    devices = lax.axis_size("expert")
    experts = devices // 2
    tok_col, quarter = tokens.shape
    topk = routes.shape[1]
    tenant_list = adapter_output_maps.shape[2]
    adapter_rank_width = adapter_output_maps.shape[3]
    hidden_halfway = adapter_output_maps.shape[4]
    rank_halfway = adapter_rank_width // 2
    capacity = 2 * tok_col * topk // experts
    half_cap = capacity // 2
    slots = devices * capacity
    upper = lax.axis_index("expert") % 2 == 1
    flat_route = routes.reshape(-1)
    expert_hot = (flat_route[:, None] == jnp.arange(experts, dtype=jnp.int32)[None, :]).astype(
        jnp.int32
    )
    earlier = jnp.cumsum(expert_hot, axis=0) - expert_hot
    position = jnp.sum(earlier * expert_hot, axis=1)
    slot_of = (flat_route * capacity + position).reshape(tok_col, topk)
    slot_range = jnp.arange(experts * capacity, dtype=jnp.int32)
    hits = (slot_range[:, None, None] == slot_of[None, :, :]).astype(jnp.float32)
    select_tok = jnp.sum(hits, axis=2)
    prob_tok = jnp.sum(hits * router_expert_weight.astype(jnp.float32)[None, :, :], axis=2)
    tenant_hot = (tenant[:, None] == jnp.arange(tenant_list, dtype=jnp.int32)[None, :]).astype(
        jnp.float32
    )
    select_bf = select_tok.astype(jnp.bfloat16)
    send_rows = jnp.dot(select_bf, tokens, preferred_element_type=jnp.float32).astype(jnp.bfloat16)
    send_grad = jnp.dot(select_bf, output_gradient, preferred_element_type=jnp.float32).astype(
        jnp.bfloat16
    )
    send_tag = jnp.dot(prob_tok, tenant_hot, precision=lax.Precision.HIGHEST).astype(jnp.bfloat16)

    def doubled(block):
        wide = block.reshape(experts, 1, capacity, block.shape[1])
        return jnp.broadcast_to(wide, (experts, 2, capacity, block.shape[1])).reshape(
            devices, capacity, block.shape[1]
        )

    got_rows, got_grad, got_tag = (
        lax.all_to_all(doubled(send_rows), "expert", split_axis=0, concat_axis=0, tiled=True),
        lax.all_to_all(doubled(send_grad), "expert", split_axis=0, concat_axis=0, tiled=True),
        lax.all_to_all(doubled(send_tag), "expert", split_axis=0, concat_axis=0, tiled=True),
    )
    input_rows = got_rows.reshape(slots, quarter)
    rows_dy = got_grad.reshape(slots, quarter)
    tags = got_tag.reshape(slots, tenant_list).astype(jnp.float32)
    tenant_mask = (tags > 0).astype(jnp.float32)
    slot_prob = jnp.sum(tags, axis=1)
    adapter_local = adapter_input_maps[0]
    adapter_other = partner(adapter_local, "expert", 0)
    low_rank, high_rank = order_halves(adapter_local, adapter_other, upper)
    adapter_cols = jnp.concatenate([low_rank, high_rank], axis=-1).reshape(
        quarter, 2 * tenant_list * adapter_rank_width
    )
    gate_output_map = adapter_output_maps[0, 0].reshape(
        tenant_list * adapter_rank_width, hidden_halfway
    )
    up_output_map = adapter_output_maps[0, 1].reshape(
        tenant_list * adapter_rank_width, hidden_halfway
    )
    gate_part = jnp.dot(input_rows, gate_weight[0], preferred_element_type=jnp.float32)
    up_part = jnp.dot(input_rows, up_weight[0], preferred_element_type=jnp.float32)
    act_part = product_trailing(rows_dy, down_weight[0])
    proj_all = jnp.dot(input_rows, adapter_cols, preferred_element_type=jnp.float32).reshape(
        slots, 2, tenant_list, adapter_rank_width
    )
    proj_part = jnp.sum(proj_all * tenant_mask[:, None, :, None], axis=2).reshape(
        slots, 2 * adapter_rank_width
    )
    gate_total, up_total, act_sum, proj_sum = lax.psum(
        (gate_part, up_part, act_part, proj_part), "dp"
    )
    proj_low = proj_sum.astype(jnp.bfloat16)
    spread_in = spread(proj_low, tenant_mask, tenant_list, adapter_rank_width)
    gate_preactivation = gate_total + ADAPTER_SCALE * jnp.dot(
        spread_in[:, 0], gate_output_map, preferred_element_type=jnp.float32
    )
    up_preactivation = up_total + ADAPTER_SCALE * jnp.dot(
        spread_in[:, 1], up_output_map, preferred_element_type=jnp.float32
    )
    act_grad = slot_prob[:, None] * act_sum
    gate_sig = jax.nn.sigmoid(gate_preactivation)
    gate_gradient = (
        act_grad * up_preactivation * gate_sig * (1.0 + gate_preactivation * (1.0 - gate_sig))
    ).astype(jnp.bfloat16)
    up_gradient = (act_grad * gate_preactivation * gate_sig).astype(jnp.bfloat16)
    gate_gradient, up_gradient, proj_low = (gate_gradient, up_gradient, proj_low)
    projection_spread = spread(proj_low, tenant_mask, tenant_list, adapter_rank_width)
    gate_output_map_gradient = ADAPTER_SCALE * product_leading(
        projection_spread[:, 0], gate_gradient
    )
    up_output_map_gradient = ADAPTER_SCALE * product_leading(projection_spread[:, 1], up_gradient)
    adapter_b_grad = jnp.stack([gate_output_map_gradient, up_output_map_gradient]).reshape(
        1, 2, tenant_list, adapter_rank_width, hidden_halfway
    )
    backward_total = ADAPTER_SCALE * jnp.stack(
        [
            product_trailing(gate_gradient, gate_output_map),
            product_trailing(up_gradient, up_output_map),
        ],
        axis=1,
    )
    back_part = jnp.sum(
        backward_total.reshape(slots, 2, tenant_list, adapter_rank_width)
        * tenant_mask[:, None, :, None],
        axis=2,
    ).reshape(slots, 2 * adapter_rank_width)
    input_part = product_trailing(gate_gradient, gate_weight[0]) + product_trailing(
        up_gradient, up_weight[0]
    )
    by_source = input_part.reshape(devices, capacity, quarter)
    first_half = by_source[:, :half_cap]
    second_half = by_source[:, half_cap:]
    keep_half = jnp.where(upper, second_half, first_half)
    give_half = jnp.where(upper, first_half, second_half)
    taken_half, back_other = partner((give_half, back_part), "expert", 0)
    input_half = keep_half + taken_half
    back_low = (back_part + back_other).astype(jnp.bfloat16)
    back_spread = spread(back_low, tenant_mask, tenant_list, adapter_rank_width)
    spread_rows = back_spread.reshape(devices, capacity, 2 * tenant_list * adapter_rank_width)
    spread_half = jnp.where(upper, spread_rows[:, half_cap:], spread_rows[:, :half_cap]).reshape(
        devices * half_cap, 2 * tenant_list * adapter_rank_width
    )
    adapter_term = product_trailing(spread_half, adapter_cols).reshape(devices, half_cap, quarter)
    slot_grad = (input_half + adapter_term).astype(jnp.bfloat16)
    spread_ranks = back_spread.reshape(slots, 2, tenant_list, adapter_rank_width)
    mine_cols = jnp.where(
        upper, spread_ranks[..., rank_halfway:], spread_ranks[..., :rank_halfway]
    ).reshape(slots, 2 * tenant_list * rank_halfway)
    adapter_a_grad = product_leading(input_rows, mine_cols).reshape(
        1, quarter, 2, tenant_list, rank_halfway
    )
    returned = lax.all_to_all(slot_grad, "expert", split_axis=0, concat_axis=0, tiled=True)
    slot_rows = returned.reshape(experts * capacity, quarter)
    input_grad = product_leading(select_bf, slot_rows).astype(jnp.bfloat16)
    return (input_grad, adapter_a_grad, adapter_b_grad)


F32 = jnp.float32
BF16 = jnp.bfloat16
VMEM = pl.BlockSpec(memory_space=pltpu.VMEM)
HBM = pl.BlockSpec(memory_space=pltpu.HBM)
LONG = 20_000_000_000


def local_call(body, outs, operands, scratch=(), flops=0, moved=0, far=0, far_outs=0):
    operands = [
        pltpu.with_memory_space_constraint(array, pltpu.HBM) if k < far else array
        for k, array in enumerate(operands)
    ]
    return pl.pallas_call(
        body,
        out_shape=[jax.ShapeDtypeStruct(shape, kind) for shape, kind in outs],
        in_specs=[HBM] * far + [VMEM] * (len(operands) - far),
        out_specs=[HBM] * far_outs + [VMEM] * (len(outs) - far_outs),
        scratch_shapes=list(scratch),
        cost_estimate=pl.CostEstimate(flops=flops, bytes_accessed=moved, transcendentals=0),
        compiler_params=pltpu.CompilerParams(vmem_limit_bytes=16 << 20),
    )(*operands)


def dot_plain(left, right):
    return lax.dot_general(left, right, (((1,), (0,)), ((), ())), preferred_element_type=F32)


def swap(array, axis, offset):
    return lax.ppermute(array, axis, [(i, i ^ offset) for i in range(lax.axis_size(axis))])


def pack_body(
    x_ref, dy_ref, routes_ref, weight_ref, tenant_ref, out_ref, routes, weight, tenant, arrived
):
    width = x_ref.shape[1]
    topk, count = routes_ref.shape
    copies = [
        pltpu.make_async_copy(source, target, arrived.at[k])
        for k, (source, target) in enumerate(
            (
                (routes_ref, routes),
                (weight_ref, weight),
                (tenant_ref, tenant),
                (x_ref, out_ref.at[:, :width]),
                (dy_ref, out_ref.at[:, width : 2 * width]),
            )
        )
    ]
    for copy in copies:
        copy.start()
    for copy in copies[:3]:
        copy.wait()
    tags = [routes[...].astype(F32), weight[...].astype(F32), tenant[...].astype(F32)]
    rows = 2 * topk + 1
    tags = jnp.concatenate(tags + [jnp.zeros((count - rows, count), F32)], axis=0)
    tags = jnp.concatenate([tags, jnp.zeros((count, 128 - count), F32)], axis=1)
    out_ref[:, 2 * width :] = tags.astype(BF16)
    for copy in copies[3:]:
        copy.wait()


def stage_body(*refs):
    count = (len(refs) - 2) // 2
    sources, targets, maps, arrived = refs[:count], refs[count : 2 * count], refs[-2], refs[-1]
    copies = [
        pltpu.make_async_copy(source, target, arrived.at[k])
        for k, (source, target) in enumerate(zip(sources, targets[:-1] + (maps,)))
    ]
    for copy in copies:
        copy.start()
    copies[-1].wait()
    targets[-1][...] = dot_plain(rank_order(maps.shape[0], False), maps[...]).astype(BF16)
    for copy in copies[:-1]:
        copy.wait()


def rank_order(lanes, columns):
    at = lax.broadcasted_iota(jnp.int32, (lanes, lanes), 0 if columns else 1)
    place = lax.broadcasted_iota(jnp.int32, (lanes, lanes), 1 if columns else 0)
    if not columns:
        at, place = place, at
    source = lax.rem(place // 8, 2) * (lanes // 2) + (place // 16) * 8 + lax.rem(place, 8)
    return (at == source).astype(BF16)


def forward_body(*refs):
    gate_ref, up_ref, down_ref, mine_ref, other_ref, total_ref = refs[-6:]
    width, hidden = gate_ref.shape
    blocks = [ref[...].astype(F32) for ref in refs[:-6]]
    upper = lax.rem(lax.axis_index("expert"), 2)
    x = jnp.concatenate([block[:, :width] for block in blocks], axis=0).astype(BF16)
    dy = jnp.concatenate([block[:, width : 2 * width] for block in blocks], axis=0).astype(BF16)
    total_ref[:, :hidden] = dot_plain(x, gate_ref[...]).astype(BF16)
    total_ref[:, hidden : 2 * hidden] = dot_plain(x, up_ref[...]).astype(BF16)
    total_ref[:, 2 * hidden : 3 * hidden] = product_trailing(dy, down_ref[...]).astype(BF16)
    mine = product_trailing(x, mine_ref[...])
    other = product_trailing(x, other_ref[...])
    low = jnp.where(upper == 1, other, mine)
    high = jnp.where(upper == 1, mine, other)
    total_ref[:, 3 * hidden :] = jnp.concatenate([low, high], axis=1).astype(BF16)


def forward_rest_body(*refs):
    before_ref, total_ref, mine_total_ref = refs[-3:]
    forward_body(*refs[:-3], total_ref)
    mine_total_ref[...] = before_ref[...]


def pair_body(own_ref, taken_ref, out_ref):
    out_ref[...] = (own_ref[...].astype(F32) + taken_ref[...].astype(F32)).astype(BF16)


def tags_body(topk, *refs):
    x_ref, tag_ref = refs[-2:]
    width = x_ref.shape[1]
    blocks = [ref[...].astype(F32) for ref in refs[:-2]]
    count = blocks[0].shape[0]
    slots = count * len(blocks)
    expert = (lax.axis_index("expert") // 2).astype(F32)
    x_ref[...] = jnp.concatenate([block[:, :width] for block in blocks], axis=0).astype(BF16)
    eye = (
        lax.broadcasted_iota(jnp.int32, (count, 128), 0)
        == lax.broadcasted_iota(jnp.int32, (count, 128), 1)
    ).astype(BF16)
    tags = jnp.concatenate(
        [product_leading(block[:, 2 * width :].astype(BF16), eye)[:count] for block in blocks],
        axis=0,
    )
    prob = jnp.zeros((slots, 1), F32)
    for k in range(topk):
        prob += jnp.where(tags[:, k : k + 1] == expert, tags[:, topk + k : topk + k + 1], 0.0)
    lane = lax.broadcasted_iota(jnp.int32, (slots, 128), 1)
    tenant = tags[:, 2 * topk : 2 * topk + 1]
    tag_ref[...] = jnp.where(lane == 0, prob, jnp.where(lane == 1, tenant, 0.0))


def lane_masks(tenant, shape, ranks):
    lane = lax.broadcasted_iota(jnp.int32, shape, 1)
    half = shape[1] // 2
    inner = lax.rem(lane, half)
    is_gate = inner < half // 2
    tenant_of = lax.rem(inner, half // 2) // ranks
    return is_gate, tenant_of.astype(F32) == tenant


def backward_rows(
    ranks,
    rows,
    total,
    tag_ref,
    gate_ref,
    up_ref,
    mine_ref,
    other_ref,
    maps_ref,
    rows_ref,
    back_ref,
):
    hidden = gate_ref.shape[1]
    half = mine_ref.shape[0]
    upper = lax.rem(lax.axis_index("expert"), 2)
    tags = tag_ref[rows, :]
    low = total[:, 3 * hidden :]
    is_gate, keep = lane_masks(tags[:, 1:2], low.shape, ranks)
    low = jnp.where(keep, low, 0.0).astype(BF16)
    low_wide = low.astype(F32)
    maps = maps_ref[...]
    gate = total[:, :hidden] + ADAPTER_SCALE * dot_plain(
        jnp.where(is_gate, low_wide, 0.0).astype(BF16), maps
    )
    up = total[:, hidden : 2 * hidden] + ADAPTER_SCALE * dot_plain(
        jnp.where(is_gate, 0.0, low_wide).astype(BF16), maps
    )
    act = tags[:, :1] * total[:, 2 * hidden : 3 * hidden]
    sig = jax.nn.sigmoid(gate)
    gate_grad = (act * up * sig * (1.0 + gate * (1.0 - sig))).astype(BF16)
    up_grad = (act * gate * sig).astype(BF16)
    rows_ref[:, :hidden] = gate_grad
    rows_ref[:, hidden : 2 * hidden] = up_grad
    rows_ref[:, 2 * hidden :] = low
    back_gate = product_trailing(gate_grad, maps)
    back_up = product_trailing(up_grad, maps)
    back = ADAPTER_SCALE * jnp.where(keep, jnp.where(is_gate, back_gate, back_up), 0.0)
    low, high = back[:, :half], back[:, half:]
    mine = jnp.where(upper == 1, high, low)
    other = jnp.where(upper == 1, low, high)
    back_ref[...] = jnp.concatenate([mine, other], axis=1)
    total = product_trailing(gate_grad, gate_ref[...])
    total += product_trailing(up_grad, up_ref[...])
    total += dot_plain(mine.astype(BF16), mine_ref[...])
    return total + dot_plain(other.astype(BF16), other_ref[...])


def backward_body(ranks, own_ref, second_ref, first_ref, third_ref, *refs):
    give_ref, rows_ref, back_ref = refs[-3:]
    count, lanes = back_ref.shape
    width = give_ref.shape[1] - lanes // 2
    total = (own_ref[...].astype(F32) + first_ref[...].astype(F32)) + (
        second_ref[...].astype(F32) + third_ref[...].astype(F32)
    )
    total = backward_rows(ranks, slice(0, count), total, *refs[:-3], rows_ref, back_ref)
    give_ref[:, :width] = total.astype(BF16)
    give_ref[:, width:] = back_ref[:, lanes // 2 :].astype(BF16)


def backward_rest_body(ranks, own_ref, pair_ref, *refs):
    keep_ref, back_give_ref, rows_ref, back_ref = refs[-4:]
    count, lanes = back_ref.shape
    total = own_ref[...].astype(F32) + pair_ref[...].astype(F32)
    keep_ref[...] = backward_rows(
        ranks, slice(count, 2 * count), total, *refs[:-4], rows_ref, back_ref
    )
    back_give_ref[...] = back_ref[:, lanes // 2 :]


def join_body(keep_ref, taken_ref, own_ref, first_ref, second_ref, third_ref):
    count = own_ref.shape[0]
    total = keep_ref[...] + taken_ref[:, : own_ref.shape[1]].astype(F32)
    for k, ref in enumerate((own_ref, first_ref, second_ref, third_ref)):
        ref[...] = total[k * count : (k + 1) * count].astype(ref.dtype)


def finish_body(own_ref, third_ref, second_ref, first_ref, out_ref):
    total = (own_ref[...] + first_ref[...].astype(F32)) + (
        second_ref[...].astype(F32) + third_ref[...].astype(F32)
    )
    out_ref[...] = total.astype(BF16)


def maps_grad_body(rows_ref, rest_rows_ref, out_ref):
    lanes, hidden = out_ref.shape
    half = lanes // 2
    rows = jnp.concatenate([rows_ref[...], rest_rows_ref[...]], axis=0)
    low = dot_plain(rows[:, 2 * hidden :], rank_order(lanes, True)).astype(BF16)
    out_ref[:half] = ADAPTER_SCALE * product_leading(low[:, :half], rows[:, :hidden])
    out_ref[half:] = ADAPTER_SCALE * product_leading(low[:, half:], rows[:, hidden : 2 * hidden])


def input_maps_grad_body(back_ref, rest_back_ref, taken_ref, rest_taken_ref, x_ref, out_ref):
    half, width = out_ref.shape
    taken = jnp.concatenate([rest_taken_ref[...], taken_ref[:, width:].astype(F32)], axis=0)
    back = jnp.concatenate([back_ref[:, :half], rest_back_ref[:, :half]], axis=0)
    out_ref[...] = product_leading((back + taken).astype(BF16), x_ref[...])


def dense_shards(
    tokens,
    output_gradient,
    routes,
    router_expert_weight,
    tenant,
    gate_weight,
    up_weight,
    down_weight,
    adapter_input_maps,
    adapter_output_maps,
):
    devices = lax.axis_size("expert")
    chips = devices // 2
    count, width = tokens.shape
    topk = routes.shape[1]
    tenants, rank, hidden = adapter_output_maps.shape[2:]
    ranks = rank // 2
    lanes = 2 * tenants * rank
    slots = devices * count
    mine_cols = adapter_input_maps[0].transpose(1, 2, 3, 0).reshape(lanes // 2, width)
    other_cols = swap(mine_cols, "expert", 1)
    (packed,) = local_call(
        pack_body,
        [((count, 2 * width + 128), BF16)],
        (tokens, output_gradient, routes.T, router_expert_weight.T, tenant[None, :]),
        scratch=[
            pltpu.VMEM((topk, count), jnp.int32),
            pltpu.VMEM((topk, count), BF16),
            pltpu.VMEM((1, count), jnp.int32),
            pltpu.SemaphoreType.DMA((5,)),
        ],
        far=5,
    )
    stored = (
        gate_weight[0],
        up_weight[0],
        down_weight[0],
        mine_cols,
        adapter_output_maps.reshape(lanes, hidden),
    )
    gate, up, down, mine_cols, maps = local_call(
        stage_body,
        [(array.shape, BF16) for array in stored],
        stored,
        scratch=[pltpu.VMEM((lanes, hidden), BF16), pltpu.SemaphoreType.DMA((len(stored),))],
        moved=sum(2 * array.size for array in stored),
        far=len(stored),
    )
    same_core = [packed] + [swap(packed, "expert", 2 * k) for k in range(1, chips)]
    same_core[-1], (gate, up, down, mine_cols, maps) = lax.optimization_barrier(
        (same_core[-1], (gate, up, down, mine_cols, maps))
    )
    other_core = [swap(block, "expert", 1) for block in same_core]
    columns = 3 * hidden + lanes
    weights = (gate, up, down, mine_cols, other_cols)
    (before,) = local_call(
        forward_body,
        [((slots // 2, columns), BF16)],
        (*same_core, *weights),
        flops=slots * width * columns,
    )
    mine, other_core = lax.optimization_barrier((before, other_core))
    (own,) = local_call(
        forward_body,
        [((slots // 2, columns), BF16)],
        (*other_core, *weights),
        flops=slots * width * columns,
    )
    sums = [own] + [swap(own, "dp", k) for k in (2, 1, 3)]
    taken = swap(mine, "dp", 2)
    (pair,) = local_call(
        pair_body,
        [((slots // 2, columns), BF16)],
        (mine, taken),
        flops=LONG,
    )
    rest_sums = [pair, swap(pair, "dp", 1)]
    blocks, _ = lax.optimization_barrier(((*other_core, *same_core), taken))
    x, tags = local_call(
        functools.partial(tags_body, topk),
        [((slots, width), BF16), ((slots, 128), F32)],
        blocks,
        flops=LONG,
    )
    shared = (tags, gate, up, mine_cols, other_cols, maps)
    outs = [((slots // 2, 2 * hidden + lanes), BF16), ((slots // 2, lanes), F32)]
    give, rows, back = local_call(
        functools.partial(backward_body, ranks),
        [((slots // 2, width + lanes // 2), BF16)] + outs,
        (*sums, *shared),
        flops=LONG,
    )
    taken = swap(give, "expert", 1)
    keep, back_give, rest_rows, rest_back = local_call(
        functools.partial(backward_rest_body, ranks),
        [((slots // 2, width), F32), ((slots // 2, lanes // 2), F32)] + outs,
        (*rest_sums, *shared),
        flops=LONG,
    )
    back_taken = swap(back_give, "expert", 1)
    own, first, second, third = local_call(
        join_body,
        [((count, width), F32)] + [((count, width), BF16)] * 3,
        (keep, taken),
    )
    third, second = swap(third, "expert", 6), swap(second, "expert", 4)
    returned = [own, third, second, swap(first, "expert", 2)]
    (maps_grad,) = local_call(maps_grad_body, [((lanes, hidden), F32)], (rows, rest_rows))
    (input_maps_grad,) = local_call(
        input_maps_grad_body,
        [((lanes // 2, width), F32)],
        (back, rest_back, taken, back_taken, x),
    )
    (input_grad,) = local_call(finish_body, [((count, width), BF16)], returned)
    adapter_a_grad = (
        input_maps_grad.reshape(2, tenants, ranks, width).transpose(3, 0, 1, 2)[None]
    )
    adapter_b_grad = maps_grad.reshape(1, 2, tenants, rank, hidden)
    return input_grad, adapter_a_grad, adapter_b_grad


def shards(*arrays):
    tokens, routes, maps = arrays[0], arrays[2], arrays[9]
    devices = lax.axis_size("expert")
    capacity = 4 * tokens.shape[0] * routes.shape[1] // devices
    if (
        capacity >= tokens.shape[0]
        and devices == 8
        and lax.axis_size("dp") == 4
        and tokens.shape[0] == 8
        and maps.shape[2] * maps.shape[3] == 64
    ):
        return dense_shards(*arrays)
    return routed_shards(*arrays)


def solution(mesh):
    placed = (
        P("expert", "dp"),
        P("expert", "dp"),
        P("expert", None),
        P("expert", None),
        P("expert"),
        P("expert", "dp", None),
        P("expert", "dp", None),
        P("expert", None, "dp"),
        P("expert", "dp", None, None, None),
        P("expert", None, None, None, None),
    )
    return jax.shard_map(
        shards,
        mesh=mesh,
        in_specs=placed,
        out_specs=(
            P("expert", "dp"),
            P("expert", "dp", None, None, None),
            P("expert", None, None, None, None),
        ),
        check_vma=False,
    )
```

```python
import functools

import jax
import jax.numpy as jnp
from jax import lax
from jax.experimental import pallas as pl
from jax.experimental.pallas import tpu as pltpu
from jax.sharding import PartitionSpec as P

ADAPTER_SCALE = 2.0


def partner(shard, axis, bit):
    return lax.ppermute(shard, axis, [(i, i ^ 1 << bit) for i in range(lax.axis_size(axis))])


def product_leading(left, right):
    return lax.dot_general(
        left, right, (((0,), (0,)), ((), ())), preferred_element_type=jnp.float32
    )


def product_trailing(left, right):
    return lax.dot_general(
        left, right, (((1,), (1,)), ((), ())), preferred_element_type=jnp.float32
    )


def order_halves(mine, other, upper):
    return (jnp.where(upper, other, mine), jnp.where(upper, mine, other))


def spread(values, tenant_mask, tenant_list, adapter_rank_width):
    count = values.shape[0]
    wide = tenant_mask[:, None, :, None] * values.astype(jnp.float32).reshape(
        count, 2, 1, adapter_rank_width
    )
    return wide.reshape(count, 2, tenant_list * adapter_rank_width).astype(jnp.bfloat16)


def routed_shards(
    tokens,
    output_gradient,
    routes,
    router_expert_weight,
    tenant,
    gate_weight,
    up_weight,
    down_weight,
    adapter_input_maps,
    adapter_output_maps,
):
    devices = lax.axis_size("expert")
    experts = devices // 2
    tok_col, quarter = tokens.shape
    topk = routes.shape[1]
    tenant_list = adapter_output_maps.shape[2]
    adapter_rank_width = adapter_output_maps.shape[3]
    hidden_halfway = adapter_output_maps.shape[4]
    rank_halfway = adapter_rank_width // 2
    capacity = 2 * tok_col * topk // experts
    half_cap = capacity // 2
    slots = devices * capacity
    upper = lax.axis_index("expert") % 2 == 1
    flat_route = routes.reshape(-1)
    expert_hot = (flat_route[:, None] == jnp.arange(experts, dtype=jnp.int32)[None, :]).astype(
        jnp.int32
    )
    earlier = jnp.cumsum(expert_hot, axis=0) - expert_hot
    position = jnp.sum(earlier * expert_hot, axis=1)
    slot_of = (flat_route * capacity + position).reshape(tok_col, topk)
    slot_range = jnp.arange(experts * capacity, dtype=jnp.int32)
    hits = (slot_range[:, None, None] == slot_of[None, :, :]).astype(jnp.float32)
    select_tok = jnp.sum(hits, axis=2)
    prob_tok = jnp.sum(hits * router_expert_weight.astype(jnp.float32)[None, :, :], axis=2)
    tenant_hot = (tenant[:, None] == jnp.arange(tenant_list, dtype=jnp.int32)[None, :]).astype(
        jnp.float32
    )
    select_bf = select_tok.astype(jnp.bfloat16)
    send_rows = jnp.dot(select_bf, tokens, preferred_element_type=jnp.float32).astype(jnp.bfloat16)
    send_grad = jnp.dot(select_bf, output_gradient, preferred_element_type=jnp.float32).astype(
        jnp.bfloat16
    )
    send_tag = jnp.dot(prob_tok, tenant_hot, precision=lax.Precision.HIGHEST).astype(jnp.bfloat16)

    def doubled(block):
        wide = block.reshape(experts, 1, capacity, block.shape[1])
        return jnp.broadcast_to(wide, (experts, 2, capacity, block.shape[1])).reshape(
            devices, capacity, block.shape[1]
        )

    got_rows, got_grad, got_tag = (
        lax.all_to_all(doubled(send_rows), "expert", split_axis=0, concat_axis=0, tiled=True),
        lax.all_to_all(doubled(send_grad), "expert", split_axis=0, concat_axis=0, tiled=True),
        lax.all_to_all(doubled(send_tag), "expert", split_axis=0, concat_axis=0, tiled=True),
    )
    input_rows = got_rows.reshape(slots, quarter)
    rows_dy = got_grad.reshape(slots, quarter)
    tags = got_tag.reshape(slots, tenant_list).astype(jnp.float32)
    tenant_mask = (tags > 0).astype(jnp.float32)
    slot_prob = jnp.sum(tags, axis=1)
    adapter_local = adapter_input_maps[0]
    adapter_other = partner(adapter_local, "expert", 0)
    low_rank, high_rank = order_halves(adapter_local, adapter_other, upper)
    adapter_cols = jnp.concatenate([low_rank, high_rank], axis=-1).reshape(
        quarter, 2 * tenant_list * adapter_rank_width
    )
    gate_output_map = adapter_output_maps[0, 0].reshape(
        tenant_list * adapter_rank_width, hidden_halfway
    )
    up_output_map = adapter_output_maps[0, 1].reshape(
        tenant_list * adapter_rank_width, hidden_halfway
    )
    gate_part = jnp.dot(input_rows, gate_weight[0], preferred_element_type=jnp.float32)
    up_part = jnp.dot(input_rows, up_weight[0], preferred_element_type=jnp.float32)
    act_part = product_trailing(rows_dy, down_weight[0])
    proj_all = jnp.dot(input_rows, adapter_cols, preferred_element_type=jnp.float32).reshape(
        slots, 2, tenant_list, adapter_rank_width
    )
    proj_part = jnp.sum(proj_all * tenant_mask[:, None, :, None], axis=2).reshape(
        slots, 2 * adapter_rank_width
    )
    gate_total, up_total, act_sum, proj_sum = lax.psum(
        (gate_part, up_part, act_part, proj_part), "dp"
    )
    proj_low = proj_sum.astype(jnp.bfloat16)
    spread_in = spread(proj_low, tenant_mask, tenant_list, adapter_rank_width)
    gate_preactivation = gate_total + ADAPTER_SCALE * jnp.dot(
        spread_in[:, 0], gate_output_map, preferred_element_type=jnp.float32
    )
    up_preactivation = up_total + ADAPTER_SCALE * jnp.dot(
        spread_in[:, 1], up_output_map, preferred_element_type=jnp.float32
    )
    act_grad = slot_prob[:, None] * act_sum
    gate_sig = jax.nn.sigmoid(gate_preactivation)
    gate_gradient = (
        act_grad * up_preactivation * gate_sig * (1.0 + gate_preactivation * (1.0 - gate_sig))
    ).astype(jnp.bfloat16)
    up_gradient = (act_grad * gate_preactivation * gate_sig).astype(jnp.bfloat16)
    gate_gradient, up_gradient, proj_low = (gate_gradient, up_gradient, proj_low)
    projection_spread = spread(proj_low, tenant_mask, tenant_list, adapter_rank_width)
    gate_output_map_gradient = ADAPTER_SCALE * product_leading(
        projection_spread[:, 0], gate_gradient
    )
    up_output_map_gradient = ADAPTER_SCALE * product_leading(projection_spread[:, 1], up_gradient)
    adapter_b_grad = jnp.stack([gate_output_map_gradient, up_output_map_gradient]).reshape(
        1, 2, tenant_list, adapter_rank_width, hidden_halfway
    )
    backward_total = ADAPTER_SCALE * jnp.stack(
        [
            product_trailing(gate_gradient, gate_output_map),
            product_trailing(up_gradient, up_output_map),
        ],
        axis=1,
    )
    back_part = jnp.sum(
        backward_total.reshape(slots, 2, tenant_list, adapter_rank_width)
        * tenant_mask[:, None, :, None],
        axis=2,
    ).reshape(slots, 2 * adapter_rank_width)
    input_part = product_trailing(gate_gradient, gate_weight[0]) + product_trailing(
        up_gradient, up_weight[0]
    )
    by_source = input_part.reshape(devices, capacity, quarter)
    first_half = by_source[:, :half_cap]
    second_half = by_source[:, half_cap:]
    keep_half = jnp.where(upper, second_half, first_half)
    give_half = jnp.where(upper, first_half, second_half)
    taken_half, back_other = partner((give_half, back_part), "expert", 0)
    input_half = keep_half + taken_half
    back_low = (back_part + back_other).astype(jnp.bfloat16)
    back_spread = spread(back_low, tenant_mask, tenant_list, adapter_rank_width)
    spread_rows = back_spread.reshape(devices, capacity, 2 * tenant_list * adapter_rank_width)
    spread_half = jnp.where(upper, spread_rows[:, half_cap:], spread_rows[:, :half_cap]).reshape(
        devices * half_cap, 2 * tenant_list * adapter_rank_width
    )
    adapter_term = product_trailing(spread_half, adapter_cols).reshape(devices, half_cap, quarter)
    slot_grad = (input_half + adapter_term).astype(jnp.bfloat16)
    spread_ranks = back_spread.reshape(slots, 2, tenant_list, adapter_rank_width)
    mine_cols = jnp.where(
        upper, spread_ranks[..., rank_halfway:], spread_ranks[..., :rank_halfway]
    ).reshape(slots, 2 * tenant_list * rank_halfway)
    adapter_a_grad = product_leading(input_rows, mine_cols).reshape(
        1, quarter, 2, tenant_list, rank_halfway
    )
    returned = lax.all_to_all(slot_grad, "expert", split_axis=0, concat_axis=0, tiled=True)
    slot_rows = returned.reshape(experts * capacity, quarter)
    input_grad = product_leading(select_bf, slot_rows).astype(jnp.bfloat16)
    return (input_grad, adapter_a_grad, adapter_b_grad)


F32 = jnp.float32
BF16 = jnp.bfloat16
VMEM = pl.BlockSpec(memory_space=pltpu.VMEM)
HBM = pl.BlockSpec(memory_space=pltpu.HBM)
LONG = 20_000_000_000


def local_call(body, outs, operands, scratch=(), flops=0, moved=0, far=0, far_outs=0):
    operands = [
        pltpu.with_memory_space_constraint(array, pltpu.HBM) if k < far else array
        for k, array in enumerate(operands)
    ]
    return pl.pallas_call(
        body,
        out_shape=[jax.ShapeDtypeStruct(shape, kind) for shape, kind in outs],
        in_specs=[HBM] * far + [VMEM] * (len(operands) - far),
        out_specs=[HBM] * far_outs + [VMEM] * (len(outs) - far_outs),
        scratch_shapes=list(scratch),
        cost_estimate=pl.CostEstimate(flops=flops, bytes_accessed=moved, transcendentals=0),
        compiler_params=pltpu.CompilerParams(vmem_limit_bytes=16 << 20),
    )(*operands)


def dot_plain(left, right):
    return lax.dot_general(left, right, (((1,), (0,)), ((), ())), preferred_element_type=F32)


def swap(array, axis, offset):
    return lax.ppermute(array, axis, [(i, i ^ offset) for i in range(lax.axis_size(axis))])


def pack_body(
    x_ref, dy_ref, routes_ref, weight_ref, tenant_ref, out_ref, routes, weight, tenant, arrived
):
    width = x_ref.shape[1]
    topk, count = routes_ref.shape
    copies = [
        pltpu.make_async_copy(source, target, arrived.at[k])
        for k, (source, target) in enumerate(
            (
                (routes_ref, routes),
                (weight_ref, weight),
                (tenant_ref, tenant),
                (x_ref, out_ref.at[:, :width]),
                (dy_ref, out_ref.at[:, width : 2 * width]),
            )
        )
    ]
    for copy in copies:
        copy.start()
    for copy in copies[:3]:
        copy.wait()
    tags = [routes[...].astype(F32), weight[...].astype(F32), tenant[...].astype(F32)]
    rows = 2 * topk + 1
    tags = jnp.concatenate(tags + [jnp.zeros((count - rows, count), F32)], axis=0)
    tags = jnp.concatenate([tags, jnp.zeros((count, 128 - count), F32)], axis=1)
    out_ref[:, 2 * width :] = tags.astype(BF16)
    for copy in copies[3:]:
        copy.wait()


def stage_body(*refs):
    count = (len(refs) - 2) // 2
    sources, targets, maps, arrived = refs[:count], refs[count : 2 * count], refs[-2], refs[-1]
    copies = [
        pltpu.make_async_copy(source, target, arrived.at[k])
        for k, (source, target) in enumerate(zip(sources, targets[:-1] + (maps,)))
    ]
    for copy in copies:
        copy.start()
    copies[-1].wait()
    targets[-1][...] = dot_plain(rank_order(maps.shape[0], False), maps[...]).astype(BF16)
    for copy in copies[:-1]:
        copy.wait()


def rank_order(lanes, columns):
    at = lax.broadcasted_iota(jnp.int32, (lanes, lanes), 0 if columns else 1)
    place = lax.broadcasted_iota(jnp.int32, (lanes, lanes), 1 if columns else 0)
    if not columns:
        at, place = place, at
    source = lax.rem(place // 8, 2) * (lanes // 2) + (place // 16) * 8 + lax.rem(place, 8)
    return (at == source).astype(BF16)


def forward_body(*refs):
    gate_ref, up_ref, down_ref, mine_ref, other_ref, total_ref = refs[-6:]
    width, hidden = gate_ref.shape
    blocks = [ref[...].astype(F32) for ref in refs[:-6]]
    upper = lax.rem(lax.axis_index("expert"), 2)
    x = jnp.concatenate([block[:, :width] for block in blocks], axis=0).astype(BF16)
    dy = jnp.concatenate([block[:, width : 2 * width] for block in blocks], axis=0).astype(BF16)
    total_ref[:, :hidden] = dot_plain(x, gate_ref[...]).astype(BF16)
    total_ref[:, hidden : 2 * hidden] = dot_plain(x, up_ref[...]).astype(BF16)
    total_ref[:, 2 * hidden : 3 * hidden] = product_trailing(dy, down_ref[...]).astype(BF16)
    mine = product_trailing(x, mine_ref[...])
    other = product_trailing(x, other_ref[...])
    low = jnp.where(upper == 1, other, mine)
    high = jnp.where(upper == 1, mine, other)
    total_ref[:, 3 * hidden :] = jnp.concatenate([low, high], axis=1).astype(BF16)


def forward_rest_body(*refs):
    before_ref, total_ref, mine_total_ref = refs[-3:]
    forward_body(*refs[:-3], total_ref)
    mine_total_ref[...] = before_ref[...]


def pair_body(own_ref, taken_ref, out_ref):
    out_ref[...] = (own_ref[...].astype(F32) + taken_ref[...].astype(F32)).astype(BF16)


def tags_body(topk, *refs):
    x_ref, tag_ref = refs[-2:]
    width = x_ref.shape[1]
    blocks = [ref[...].astype(F32) for ref in refs[:-2]]
    count = blocks[0].shape[0]
    slots = count * len(blocks)
    expert = (lax.axis_index("expert") // 2).astype(F32)
    x_ref[...] = jnp.concatenate([block[:, :width] for block in blocks], axis=0).astype(BF16)
    eye = (
        lax.broadcasted_iota(jnp.int32, (count, 128), 0)
        == lax.broadcasted_iota(jnp.int32, (count, 128), 1)
    ).astype(BF16)
    tags = jnp.concatenate(
        [product_leading(block[:, 2 * width :].astype(BF16), eye)[:count] for block in blocks],
        axis=0,
    )
    prob = jnp.zeros((slots, 1), F32)
    for k in range(topk):
        prob += jnp.where(tags[:, k : k + 1] == expert, tags[:, topk + k : topk + k + 1], 0.0)
    lane = lax.broadcasted_iota(jnp.int32, (slots, 128), 1)
    tenant = tags[:, 2 * topk : 2 * topk + 1]
    tag_ref[...] = jnp.where(lane == 0, prob, jnp.where(lane == 1, tenant, 0.0))


def lane_masks(tenant, shape, ranks):
    lane = lax.broadcasted_iota(jnp.int32, shape, 1)
    half = shape[1] // 2
    inner = lax.rem(lane, half)
    is_gate = inner < half // 2
    tenant_of = lax.rem(inner, half // 2) // ranks
    return is_gate, tenant_of.astype(F32) == tenant


def backward_rows(
    ranks,
    rows,
    total,
    tag_ref,
    gate_ref,
    up_ref,
    mine_ref,
    other_ref,
    maps_ref,
    rows_ref,
    back_ref,
):
    hidden = gate_ref.shape[1]
    half = mine_ref.shape[0]
    upper = lax.rem(lax.axis_index("expert"), 2)
    tags = tag_ref[rows, :]
    low = total[:, 3 * hidden :]
    is_gate, keep = lane_masks(tags[:, 1:2], low.shape, ranks)
    low = jnp.where(keep, low, 0.0).astype(BF16)
    low_wide = low.astype(F32)
    maps = maps_ref[...]
    gate = total[:, :hidden] + ADAPTER_SCALE * dot_plain(
        jnp.where(is_gate, low_wide, 0.0).astype(BF16), maps
    )
    up = total[:, hidden : 2 * hidden] + ADAPTER_SCALE * dot_plain(
        jnp.where(is_gate, 0.0, low_wide).astype(BF16), maps
    )
    act = tags[:, :1] * total[:, 2 * hidden : 3 * hidden]
    sig = jax.nn.sigmoid(gate)
    gate_grad = (act * up * sig * (1.0 + gate * (1.0 - sig))).astype(BF16)
    up_grad = (act * gate * sig).astype(BF16)
    rows_ref[:, :hidden] = gate_grad
    rows_ref[:, hidden : 2 * hidden] = up_grad
    rows_ref[:, 2 * hidden :] = low
    back_gate = product_trailing(gate_grad, maps)
    back_up = product_trailing(up_grad, maps)
    back = ADAPTER_SCALE * jnp.where(keep, jnp.where(is_gate, back_gate, back_up), 0.0)
    low, high = back[:, :half], back[:, half:]
    mine = jnp.where(upper == 1, high, low)
    other = jnp.where(upper == 1, low, high)
    back_ref[...] = jnp.concatenate([mine, other], axis=1)
    total = product_trailing(gate_grad, gate_ref[...])
    total += product_trailing(up_grad, up_ref[...])
    total += dot_plain(mine.astype(BF16), mine_ref[...])
    return total + dot_plain(other.astype(BF16), other_ref[...])


def backward_body(ranks, own_ref, second_ref, first_ref, third_ref, *refs):
    give_ref, rows_ref, back_ref = refs[-3:]
    count, lanes = back_ref.shape
    width = give_ref.shape[1] - lanes // 2
    total = (own_ref[...].astype(F32) + first_ref[...].astype(F32)) + (
        second_ref[...].astype(F32) + third_ref[...].astype(F32)
    )
    total = backward_rows(ranks, slice(0, count), total, *refs[:-3], rows_ref, back_ref)
    give_ref[:, :width] = total
    give_ref[:, width:] = back_ref[:, lanes // 2 :]


def backward_rest_body(ranks, own_ref, pair_ref, *refs):
    keep_ref, back_give_ref, rows_ref, back_ref = refs[-4:]
    count, lanes = back_ref.shape
    total = own_ref[...].astype(F32) + pair_ref[...].astype(F32)
    keep_ref[...] = backward_rows(
        ranks, slice(count, 2 * count), total, *refs[:-4], rows_ref, back_ref
    )
    back_give_ref[...] = back_ref[:, lanes // 2 :]


def join_body(keep_ref, taken_ref, own_ref, first_ref, second_ref, third_ref):
    count = own_ref.shape[0]
    total = keep_ref[...] + taken_ref[:, : own_ref.shape[1]].astype(F32)
    for k, ref in enumerate((own_ref, first_ref, second_ref, third_ref)):
        ref[...] = total[k * count : (k + 1) * count].astype(ref.dtype)


def finish_body(own_ref, third_ref, second_ref, first_ref, out_ref):
    total = (own_ref[...] + first_ref[...].astype(F32)) + (
        second_ref[...].astype(F32) + third_ref[...].astype(F32)
    )
    out_ref[...] = total.astype(BF16)


def maps_grad_body(rows_ref, rest_rows_ref, out_ref):
    lanes, hidden = out_ref.shape
    half = lanes // 2
    rows = jnp.concatenate([rows_ref[...], rest_rows_ref[...]], axis=0)
    low = dot_plain(rows[:, 2 * hidden :], rank_order(lanes, True)).astype(BF16)
    out_ref[:half] = ADAPTER_SCALE * product_leading(low[:, :half], rows[:, :hidden])
    out_ref[half:] = ADAPTER_SCALE * product_leading(low[:, half:], rows[:, hidden : 2 * hidden])


def input_maps_grad_body(back_ref, rest_back_ref, taken_ref, rest_taken_ref, x_ref, out_ref):
    half, width = out_ref.shape
    taken = jnp.concatenate([rest_taken_ref[...], taken_ref[:, width:].astype(F32)], axis=0)
    back = jnp.concatenate([back_ref[:, :half], rest_back_ref[:, :half]], axis=0)
    out_ref[...] = product_leading((back + taken).astype(BF16), x_ref[...])


def dense_shards(
    tokens,
    output_gradient,
    routes,
    router_expert_weight,
    tenant,
    gate_weight,
    up_weight,
    down_weight,
    adapter_input_maps,
    adapter_output_maps,
):
    devices = lax.axis_size("expert")
    chips = devices // 2
    count, width = tokens.shape
    topk = routes.shape[1]
    tenants, rank, hidden = adapter_output_maps.shape[2:]
    ranks = rank // 2
    lanes = 2 * tenants * rank
    slots = devices * count
    mine_cols = adapter_input_maps[0].transpose(1, 2, 3, 0).reshape(lanes // 2, width)
    (packed,) = local_call(
        pack_body,
        [((count, 2 * width + 128), BF16)],
        (tokens, output_gradient, routes.T, router_expert_weight.T, tenant[None, :]),
        scratch=[
            pltpu.VMEM((topk, count), jnp.int32),
            pltpu.VMEM((topk, count), BF16),
            pltpu.VMEM((1, count), jnp.int32),
            pltpu.SemaphoreType.DMA((5,)),
        ],
        far=5,
    )
    packed, late_cols = lax.optimization_barrier((packed, mine_cols))
    other_cols = swap(late_cols, "expert", 1)
    stored = (
        gate_weight[0],
        up_weight[0],
        down_weight[0],
        mine_cols,
        adapter_output_maps.reshape(lanes, hidden),
    )
    gate, up, down, mine_cols, maps = local_call(
        stage_body,
        [(array.shape, BF16) for array in stored],
        stored,
        scratch=[pltpu.VMEM((lanes, hidden), BF16), pltpu.SemaphoreType.DMA((len(stored),))],
        moved=sum(2 * array.size for array in stored),
        far=len(stored),
    )
    same_core = [packed] + [swap(packed, "expert", 2 * k) for k in range(1, chips)]
    same_core[-1], (gate, up, down, mine_cols, maps) = lax.optimization_barrier(
        (same_core[-1], (gate, up, down, mine_cols, maps))
    )
    other_core = [swap(block, "expert", 1) for block in same_core]
    columns = 3 * hidden + lanes
    weights = (gate, up, down, mine_cols, other_cols)
    (before,) = local_call(
        forward_body,
        [((slots // 2, columns), BF16)],
        (*same_core, *weights),
        flops=slots * width * columns,
    )
    mine, other_core = lax.optimization_barrier((before, other_core))
    (own,) = local_call(
        forward_body,
        [((slots // 2, columns), BF16)],
        (*other_core, *weights),
        flops=slots * width * columns,
    )
    sums = [own] + [swap(own, "dp", k) for k in (2, 1, 3)]
    taken = swap(mine, "dp", 2)
    (pair,) = local_call(
        pair_body,
        [((slots // 2, columns), BF16)],
        (mine, taken),
        flops=LONG,
    )
    rest_sums = [pair, swap(pair, "dp", 1)]
    blocks, _ = lax.optimization_barrier(((*other_core, *same_core), taken))
    x, tags = local_call(
        functools.partial(tags_body, topk),
        [((slots, width), BF16), ((slots, 128), F32)],
        blocks,
        flops=LONG,
    )
    shared = (tags, gate, up, mine_cols, other_cols, maps)
    outs = [((slots // 2, 2 * hidden + lanes), BF16), ((slots // 2, lanes), F32)]
    give, rows, back = local_call(
        functools.partial(backward_body, ranks),
        [((slots // 2, width + lanes // 2), F32)] + outs,
        (*sums, *shared),
        flops=LONG,
    )
    taken = swap(give, "expert", 1)
    keep, back_give, rest_rows, rest_back = local_call(
        functools.partial(backward_rest_body, ranks),
        [((slots // 2, width), F32), ((slots // 2, lanes // 2), F32)] + outs,
        (*rest_sums, *shared),
        flops=LONG,
    )
    back_taken = swap(back_give, "expert", 1)
    own, first, second, third = local_call(
        join_body,
        [((count, width), F32)] + [((count, width), BF16)] * 3,
        (keep, taken),
    )
    third, second = swap(third, "expert", 6), swap(second, "expert", 4)
    returned = [own, third, second, swap(first, "expert", 2)]
    (maps_grad,) = local_call(maps_grad_body, [((lanes, hidden), F32)], (rows, rest_rows))
    (input_maps_grad,) = local_call(
        input_maps_grad_body,
        [((lanes // 2, width), F32)],
        (back, rest_back, taken, back_taken, x),
    )
    (input_grad,) = local_call(finish_body, [((count, width), BF16)], returned)
    adapter_a_grad = (
        input_maps_grad.reshape(2, tenants, ranks, width).transpose(3, 0, 1, 2)[None]
    )
    adapter_b_grad = maps_grad.reshape(1, 2, tenants, rank, hidden)
    return input_grad, adapter_a_grad, adapter_b_grad


def shards(*arrays):
    tokens, routes, maps = arrays[0], arrays[2], arrays[9]
    devices = lax.axis_size("expert")
    capacity = 4 * tokens.shape[0] * routes.shape[1] // devices
    if (
        capacity >= tokens.shape[0]
        and devices == 8
        and lax.axis_size("dp") == 4
        and tokens.shape[0] == 8
        and maps.shape[2] * maps.shape[3] == 64
    ):
        return dense_shards(*arrays)
    return routed_shards(*arrays)


def solution(mesh):
    placed = (
        P("expert", "dp"),
        P("expert", "dp"),
        P("expert", None),
        P("expert", None),
        P("expert"),
        P("expert", "dp", None),
        P("expert", "dp", None),
        P("expert", None, "dp"),
        P("expert", "dp", None, None, None),
        P("expert", None, None, None, None),
    )
    return jax.shard_map(
        shards,
        mesh=mesh,
        in_specs=placed,
        out_specs=(
            P("expert", "dp"),
            P("expert", "dp", None, None, None),
            P("expert", None, None, None, None),
        ),
        check_vma=False,
    )
```
